512 devices in a mesh: section: 8 (over y, z_hi), dp: 64 (over z_lo, x, core).
Axes of the slice: x: 4, y: 4, z: 16 (z_hi: 2, z_lo: 8; z = z_hi * 8 + z_lo), core: 2. Of those that a mesh axis runs over, the one named last changes fastest.
Arguments:
- images: bfloat16 [256, 128, 1664], P('dp'), may hold values from -6 to 6
- text_pooled: bfloat16 [256, 1280], P('dp'), may hold values from -6 to 6
- image_weight: bfloat16 [8, 1664, 1664], P('section', 'dp'), may hold values from -0.15625 to 0.15625
- proj_image: bfloat16 [1664, 1280], P(None, 'dp'), may hold values from -0.15625 to 0.15625
- proj_text: bfloat16 [1280, 1280], P(None, 'dp'), may hold values from -0.15625 to 0.15625
- logit_scale: float32 [1], replicated, may hold values from 20 to 60
- pairing: int32 [256], replicated, may hold values from 0 to 255, each once
Outputs:
- logits: float32 [256, 256], P('dp', 'section')
- image_loss: float32 [256], P('dp')
- text_loss: float32 [256], P('dp')
The draws below stay inside these ranges and needn't reach their ends.
Inputs may be any that keep to these rules, and one draw needn't show every extreme that they name: `pairing`: each caption index appears exactly once.
All inputs are finite; a program needn't handle non-finite values.
Results may differ from the reference program's by a relative error of at most 0.02.
Values may be sent and summed in bfloat16 or wider, within the bound.
No kernel may reach another device: no remote copies, remote signals or barrier semaphores. Data moves between devices by JAX's collectives and lax.ppermute only.
A program may use at most 64 MiB of HBM per device.

```python
import math
import jax
import jax.numpy as jnp
from jax import lax

D_I = 1664
D_T = 1280
EMB = 1280
TOK_I = 128
LAYERS = 8
GB = 256


def block_scale(rng, extent, pieces, least, high):
    loudness = 1.0
    for position, shards_of in pieces:
        steps = jax.random.uniform(jax.random.fold_in(jax.random.fold_in(rng, 6), position), (shards_of,), jnp.float32, least / len(pieces), high / len(pieces))
        loudness = loudness * jnp.repeat(jnp.exp(steps), extent[position] // shards_of).reshape((-1,) + (1,) * (len(extent) - 1 - position))
    return loudness


def centred(stream_key, shape, scale, most, shards=(), kind=jnp.bfloat16):
    result = scale * jax.random.normal(stream_key, shape, jnp.float32)
    if shards:
        result = result * block_scale(stream_key, shape, shards, -0.22, 0.18)
    return jnp.clip(result, -most, most).astype(kind)


def setup_inputs(seed: int = 0) -> dict:
    streams_of = jax.random.split(jax.random.key(seed), 8)
    return {
        "images": centred(streams_of[0], (GB, TOK_I, D_I), 1.0, 6.0, ((0, 64),)),
        "text_pooled": centred(streams_of[1], (GB, D_T), 1.0, 6.0, ((0, 64),)),
        "image_weight": centred(streams_of[2], (LAYERS, D_I, D_I), D_I ** -0.5, 0.15625, ((0, 8), (1, 64))),
        "proj_image": centred(streams_of[3], (D_I, EMB), D_I ** -0.5, 0.15625, ((1, 64),)),
        "proj_text": centred(streams_of[4], (D_T, EMB), D_T ** -0.5, 0.15625, ((1, 64),)),
        "logit_scale": jnp.clip(jnp.exp(jax.random.uniform(streams_of[5], (1,), jnp.float32, math.log(20.0), math.log(60.0))), 20.0, 60.0),
        "pairing": jax.random.permutation(streams_of[6], GB).astype(jnp.int32),
    }


def normalize(values_in):
    values_in = values_in.astype(jnp.float32)
    center = lax.optimization_barrier(jnp.mean(values_in, axis=-1, keepdims=True))
    spread = lax.optimization_barrier(jnp.mean((values_in - center) ** 2, axis=-1, keepdims=True))
    return (values_in - center) / jnp.sqrt(spread + 1e-05)

def reference(images, text_pooled, image_weight, proj_image, proj_text, logit_scale, pairing):
    count = images.shape[0]
    tokens = images.shape[1]
    width = images.shape[2]
    activ = images.reshape(count * tokens, width)
    for depth in range(LAYERS):
        normed = normalize(activ).astype(jnp.bfloat16)
        update = jnp.dot(normed, image_weight[depth], preferred_element_type=jnp.float32)
        activ = (activ.astype(jnp.float32) + jax.nn.gelu(update)).astype(jnp.bfloat16)
    pooled_image = lax.optimization_barrier(jnp.mean(normalize(activ).reshape(count, tokens, width), axis=1)).astype(jnp.bfloat16)
    img_emb = jnp.dot(pooled_image, proj_image, preferred_element_type=jnp.float32)
    text_emb = jnp.dot(text_pooled, proj_text, preferred_element_type=jnp.float32)
    img_unit = (img_emb / jnp.sqrt(lax.optimization_barrier(jnp.sum(img_emb * img_emb, axis=1, keepdims=True)) + 1e-06)).astype(jnp.bfloat16)
    text_unit = (text_emb / jnp.sqrt(lax.optimization_barrier(jnp.sum(text_emb * text_emb, axis=1, keepdims=True)) + 1e-06)).astype(jnp.bfloat16)
    logits = logit_scale[0] * jnp.dot(img_unit, text_unit.T, preferred_element_type=jnp.float32)
    positive = jnp.take_along_axis(logits, pairing[:, None].astype(jnp.int32), axis=1)[:, 0]
    image_loss = jnp.log(lax.optimization_barrier(jnp.sum(jnp.exp(logits), axis=1))) - positive
    column_lse = jnp.log(lax.optimization_barrier(jnp.sum(jnp.exp(logits), axis=0)))
    text_loss = jnp.take(column_lse, pairing) - positive
    return (logits, image_loss, text_loss)
```

```python
import functools

import jax
import jax.numpy as jnp
from jax import lax
from jax.experimental import pallas as pl
from jax.experimental.pallas import tpu as pltpu
from jax.sharding import Mesh, PartitionSpec as P

AXES = ("y", "zh", "zl", "x", "c")
SIZES = (4, 2, 8, 4, 2)
CHIPS = ("y", "zh", "zl", "x")
Z = ("zh", "zl")
bf16, f32 = jnp.bfloat16, jnp.float32


def shift(value, axis, steps):
    count = lax.axis_size(axis)
    return lax.ppermute(value, axis, [(i, (i + steps) % count) for i in range(count)])


def swap(value):
    return lax.ppermute(value, "c", [(0, 1), (1, 0)])


def normalize(values):
    values = values.astype(f32)
    center = jnp.mean(values, axis=-1, keepdims=True)
    spread = jnp.mean((values - center) ** 2, axis=-1, keepdims=True)
    return (values - center) / jnp.sqrt(spread + 1e-05)


def feature_order(rows, head):
    width = rows * 64
    tail = rows - head
    natural = lax.broadcasted_iota(jnp.int32, (width, 1), 0)
    row = natural % rows
    core = (natural // rows) % 2
    x = (natural // (rows * 2)) % 4
    zl = natural // (rows * 8)
    first = (x * 2 + core) * (8 * head) + zl * head + row
    second = 64 * head + zl * (8 * tail) + (core * 4 + x) * tail + row - head
    place = jnp.where(row < head, first, second)
    return (place == lax.broadcasted_iota(jnp.int32, (1, width), 1)).astype(bf16)


def place_of(x, y, ox, oy, head):
    from_x, from_y = (x + ox) % 4, (y + oy) % 4
    return from_y % 2, (from_x * 2 + from_y // 2) * (8 * head)


def tower_kernel(head, tail, place_ref, act_ref, *refs):
    by_y, by_x, ring, out_ref, pooled_ref, weight, normed, sems = (
        refs[0:5], refs[5:10], refs[10], refs[11], refs[12], refs[13], refs[14], refs[15]
    )
    x, y = place_ref[0], place_ref[1]
    rows = 8 * head
    width = act_ref.shape[1]

    def fetch(source, layer, first, count):
        pltpu.make_async_copy(
            source, weight.at[layer, pl.ds(pl.multiple_of(first, 16), count), :], sems.at[layer]
        ).start()

    for zh in range(2):
        for pair in range(2):
            for zl in range(8):
                fetch(
                    ring.at[zh * 8 + zl, pl.ds(pair * 8 * tail, 8 * tail), :],
                    2 * pair + zh, 8 * rows + zl * 8 * tail, 8 * tail,
                )
        own, one, two_a, two_b, three = by_y if zh == 0 else by_x
        for outer in range(4):
            for inner in range(4):
                source = (
                    own.at[inner], one.at[inner],
                    two_a.at[inner] if inner < 2 else two_b.at[inner - 2], three.at[inner],
                )[outer]
                ox, oy = (inner, outer) if zh == 0 else (outer, inner)
                pair, first = place_of(x, y, ox, oy, head)
                fetch(source, 2 * pair + zh, first, rows)

    out_ref[...] = act_ref[...]

    def layer_step(layer, carry):
        normed[...] = normalize(out_ref[...]).astype(bf16)
        pltpu.make_async_copy(weight.at[layer], weight.at[layer], sems.at[layer]).wait()
        for start in range(0, width, 256):
            cols = pl.ds(start, min(256, width - start))
            update = jnp.dot(normed[...], weight[layer, :, cols], preferred_element_type=f32)
            out_ref[:, cols] = (out_ref[:, cols].astype(f32) + jax.nn.gelu(update)).astype(bf16)
        return carry

    lax.fori_loop(0, 4, layer_step, 0)
    pooled_ref[...] = jnp.mean(normalize(out_ref[...]), axis=0, keepdims=True)


def tower(act, pieces, place, head, tail):
    tokens, width = act.shape
    vmem, anywhere = pl.BlockSpec(memory_space=pltpu.VMEM), pl.BlockSpec(memory_space=pl.ANY)
    return pl.pallas_call(
        functools.partial(tower_kernel, head, tail),
        out_shape=(
            jax.ShapeDtypeStruct((tokens, width), bf16),
            jax.ShapeDtypeStruct((1, width), f32),
        ),
        in_specs=[pl.BlockSpec(memory_space=pltpu.SMEM), vmem] + [anywhere] * 11,
        out_specs=(vmem, vmem),
        scratch_shapes=[
            pltpu.VMEM((4, width, width), bf16),
            pltpu.VMEM((tokens, width), bf16),
            pltpu.SemaphoreType.DMA((4,)),
        ],
        compiler_params=pltpu.CompilerParams(vmem_limit_bytes=40 * 1024 * 1024),
        cost_estimate=pl.CostEstimate(
            flops=8 * tokens * width * width, bytes_accessed=8 * width * width, transcendentals=0
        ),
    )(place, act, *pieces)


def gather_plane(block, axis_one, axis_two):
    near = (block, shift(block, axis_one, -1), shift(block, axis_one, 2), shift(block, axis_one, 1))
    stack = jnp.stack(near)
    one, three = shift(stack, axis_two, -1), shift(stack, axis_two, 1)
    two_a, two_b = shift(one[:2], axis_two, -1), shift(three[2:], axis_two, 1)
    return stack, one, two_a, two_b, three


def gather_ring(block, position):
    near = {0: block}
    for ahead in (4, 8, 12):
        near[ahead] = shift(block, Z, -ahead)
    stack = jnp.stack([near[ahead] for ahead in (0, 4, 8, 12)])
    one, three = shift(stack, Z, -1), shift(stack, Z, 1)
    two_a = shift(jnp.stack([near[0], near[4]]), Z, -2)
    two_b = shift(jnp.stack([near[0], near[12]]), Z, 2)
    ahead = {}
    for k in range(4):
        ahead[4 * k] = stack[k]
        ahead[4 * k + 1] = one[k]
        ahead[(4 * k + 15) % 16] = three[k]
    ahead[2], ahead[6], ahead[14], ahead[10] = two_a[0], two_a[1], two_b[0], two_b[1]
    line = jnp.stack([ahead[k % 16] for k in range(32)])
    return lax.dynamic_slice_in_dim(line, (16 - position) % 16, 16, 0)


def on_device(images, text_pooled, image_weight, proj_image, proj_text, logit_scale, pairing):
    y, zh, zl, x, c = (lax.axis_index(name) for name in AXES)
    rows = image_weight.shape[1]
    width, text_width = proj_image.shape[0], proj_text.shape[0]
    micro = images.shape[0]
    head = 18 if rows == 26 else rows // 2
    tail = rows - head
    share = proj_image.shape[1] // 4
    section = y * 2 + zh
    within = section % 4
    at_home = (y // 2) == c

    order = feature_order(rows, head)

    def ordered(values):
        return jnp.dot(values, order, preferred_element_type=f32).astype(bf16)

    weight = ordered(image_weight[0])
    crossing = [(p * 2 + 1, (p + 2) * 2) for p in (0, 1)] + [(p * 2, (p - 2) * 2 + 1) for p in (2, 3)]
    weight = jnp.where(at_home, weight, lax.ppermute(weight, ("y", "c"), crossing))

    def share_of(projection):
        return lax.dynamic_slice_in_dim(projection, within * share, share, 1).T

    text_row = lax.dynamic_slice_in_dim(text_pooled, within, 1, 0)
    widen = ((0, 0), (0, width - text_width))
    text_rows = jnp.pad(jnp.concatenate([share_of(proj_text), text_row]), widen)
    image_rows = jnp.pad(ordered(share_of(proj_image)), ((0, 1), (0, 0)))
    first_core = c == 0
    extra = jnp.where(
        at_home,
        jnp.where(first_core, text_rows, image_rows),
        swap(jnp.where(first_core, image_rows, text_rows)),
    )
    image = ordered(lax.dynamic_index_in_dim(images, within, 0, False))
    image = jnp.where(at_home, image, swap(image))

    small = jnp.concatenate([weight[head:], extra])
    spread = lax.all_to_all(
        jnp.broadcast_to(small[None], (16,) + small.shape), ("y", "x"), 0, 0, tiled=True
    )
    weight_part = spread[:, :tail].reshape(2, 2, 4, tail, width).transpose(1, 0, 2, 3, 4)
    plane_rows = jnp.concatenate([
        weight_part.reshape(16 * tail, width),
        spread[:, tail:tail + share].reshape(16 * share, width),
        spread[:, tail + share],
    ])
    ring = lax.all_gather(plane_rows, Z, axis=0)

    column = gather_ring(weight[:head], zh * 8 + zl).reshape(2, 8 * head, width)
    by_y = gather_plane(column[0], "x", "y")
    by_x = gather_plane(column[1], "y", "x")
    pieces = (*by_y, *by_x, ring)

    contract = (((1,), (1,)), ((), ()))
    projection = ring[:, 16 * tail:16 * (tail + share)].reshape(256 * share, width)
    texts = ring[:, 16 * (tail + share):, :text_width].reshape(2, 8, 2, 2, 4, text_width)
    texts = texts.transpose(1, 4, 2, 3, 0, 5).reshape(256, text_width)
    text_emb = lax.dot_general(texts, projection[:, :text_width], contract, preferred_element_type=f32)
    text_square = jnp.sum(text_emb * text_emb, axis=1, keepdims=True)
    text_unit = swap((text_emb / jnp.sqrt(text_square + 1e-06)).astype(bf16))

    place = jnp.stack([x, y]).astype(jnp.int32)
    act, _ = tower(image, pieces, place, head, tail)
    _, pooled = tower(swap(act), pieces, place, head, tail)
    image_emb = lax.dot_general(pooled.astype(bf16), projection, contract, preferred_element_type=f32)
    image_square = jnp.sum(image_emb * image_emb, axis=1, keepdims=True)
    image_unit = (image_emb / jnp.sqrt(image_square + 1e-06)).astype(bf16)
    row = logit_scale[0] * lax.dot_general(image_unit, text_unit, contract, preferred_element_type=f32)
    row = jnp.where(first_core, swap(row), row)

    count = row.shape[1]
    logits = lax.all_to_all(jnp.broadcast_to(row[None], (256, 1, count)), CHIPS, 0, 0, tiled=True)
    logits = logits.reshape(2, 2, 2, 8, 4, count).transpose(3, 4, 0, 1, 2, 5).reshape(256, count)
    row_start = ((zl * 4 + x) * 2 + c) * micro
    own_logits = lax.dynamic_slice_in_dim(logits, row_start, micro, 0)
    column_lse = jnp.log(jnp.sum(jnp.exp(logits), axis=0))
    own_pairs = lax.dynamic_slice_in_dim(pairing, row_start, micro, 0)
    paired = own_pairs[:, None] == lax.broadcasted_iota(jnp.int32, (1, count), 1)
    positive = jnp.sum(jnp.where(paired, own_logits, 0.0), axis=1)
    image_loss = jnp.log(jnp.sum(jnp.exp(own_logits), axis=1)) - positive
    text_loss = jnp.sum(jnp.where(paired, column_lse[None, :], 0.0), axis=1) - positive
    columns = count // 8
    logit_block = lax.dynamic_slice_in_dim(own_logits, section * columns, columns, 1)
    return (logit_block, image_loss, text_loss)


def solution(mesh):
    fine = Mesh(mesh.devices.reshape(SIZES), AXES)
    section, dp = ("y", "zh"), ("zl", "x", "c")
    in_specs = (
        P(dp, None, None),
        P(dp, None),
        P(section, dp, None),
        P(None, dp),
        P(None, dp),
        P(),
        P(),
    )
    out_specs = (P(dp, section), P(dp), P(dp))
    return jax.shard_map(on_device, mesh=fine, in_specs=in_specs, out_specs=out_specs, check_vma=False)
```

```python
import functools

import jax
import jax.numpy as jnp
from jax import lax
from jax.experimental import pallas as pl
from jax.experimental.pallas import tpu as pltpu
from jax.sharding import Mesh, PartitionSpec as P

AXES = ("y", "zh", "zl", "x", "c")
SIZES = (4, 2, 8, 4, 2)
CHIPS = ("y", "zh", "zl", "x")
Z = ("zh", "zl")
bf16, f32 = jnp.bfloat16, jnp.float32


def swap(value):
    return lax.ppermute(value, "c", [(0, 1), (1, 0)])


def normalize(values):
    values = values.astype(f32)
    center = jnp.mean(values, axis=-1, keepdims=True)
    spread = jnp.mean((values - center) ** 2, axis=-1, keepdims=True)
    return (values - center) / jnp.sqrt(spread + 1e-05)


def feature_order(rows, head):
    width = rows * 64
    tail = rows - head
    natural = lax.broadcasted_iota(jnp.int32, (width, 1), 0)
    row = natural % rows
    core = (natural // rows) % 2
    x = (natural // (rows * 2)) % 4
    zl = natural // (rows * 8)
    first = (x * 2 + core) * (8 * head) + zl * head + row
    second = 64 * head + zl * (8 * tail) + (core * 4 + x) * tail + row - head
    place = jnp.where(row < head, first, second)
    return (place == lax.broadcasted_iota(jnp.int32, (1, width), 1)).astype(bf16)


def fetch(source, target, sem):
    copy = pltpu.make_async_copy(source, target, sem)
    copy.start()
    return copy


def fetch_extra(ring_ref, first, share, proj, texts, sem):
    copies = []
    for z in range(16):
        rows = 16 * share
        copies.append(fetch(ring_ref.at[z, pl.ds(first, rows), :], proj.at[pl.ds(z * rows, rows), :], sem))
        if texts is not None:
            copies.append(fetch(
                ring_ref.at[z, pl.ds(first + rows, 16), :], texts.at[pl.ds(z * 16, 16), :], sem
            ))
    return copies


NT = (((1,), (1,)), ((), ()))


def unit_rows(emb):
    square = jnp.sum(emb * emb, axis=1, keepdims=True)
    return (emb / jnp.sqrt(square + 1e-06)).astype(bf16)


def texts_kernel(first, share, ring_ref, out_ref, proj, texts, sem):
    for copy in fetch_extra(ring_ref, first, share, proj, texts, sem):
        copy.wait()
    count, width = out_ref.shape
    emb = lax.dot_general(texts[:, :width], proj[:, :width], NT, preferred_element_type=f32)
    held = lax.broadcasted_iota(jnp.int32, (count, count), 1)
    zh, zl, y, x = held >> 7, (held >> 4) & 7, (held >> 2) & 3, held & 3
    index = zl * 32 + x * 8 + (y >> 1) * 4 + (y & 1) * 2 + zh
    order = (index == lax.broadcasted_iota(jnp.int32, (count, count), 0)).astype(bf16)
    out_ref[...] = jnp.dot(order, unit_rows(emb), preferred_element_type=f32).astype(bf16)


def text_units(ring, first, share, count, text_width):
    width = ring.shape[2]
    return pl.pallas_call(
        functools.partial(texts_kernel, first, share),
        out_shape=jax.ShapeDtypeStruct((count, text_width), bf16),
        in_specs=[pl.BlockSpec(memory_space=pl.ANY)],
        out_specs=pl.BlockSpec(memory_space=pltpu.VMEM),
        scratch_shapes=[
            pltpu.VMEM((256 * share, width), bf16),
            pltpu.VMEM((count, width), bf16),
            pltpu.SemaphoreType.DMA,
        ],
        compiler_params=pltpu.CompilerParams(vmem_limit_bytes=32 * 1024 * 1024),
        cost_estimate=pl.CostEstimate(
            flops=2 * count * text_width * text_width,
            bytes_accessed=512 * share * width, transcendentals=0,
        ),
    )(ring)


def tower_kernel(head, tail, share, last, place_ref, act_ref, *refs):
    pieces, ring, refs = refs[:16], refs[16], refs[17:]
    if last:
        scale_ref, units_ref, row_ref, act, weight, normed, sems, proj, extra_sem = refs
    else:
        act, weight, normed, sems = refs
    x, y, sign = place_ref[0], place_ref[1], place_ref[2]
    rows = 8 * head
    width = act_ref.shape[1]

    for zh in range(2):
        for pair in range(2):
            layer = 2 * pair + zh
            for zl in range(8):
                fetch(
                    ring.at[zh * 8 + zl, pl.ds(pair * 8 * tail, 8 * tail), :],
                    weight.at[layer, pl.ds(8 * rows + zl * 8 * tail, 8 * tail), :],
                    sems.at[layer],
                )
        for inner in range(4):
            for outer in range(4):
                source = pieces[zh * 8 + (inner // 2) * 4 + outer].at[inner % 2]
                by_x, by_y = (inner, outer) if zh == 0 else (outer, inner)
                from_x, from_y = (x + 4 + sign * by_x) % 4, (y + 4 + sign * by_y) % 4
                layer = 2 * (from_y % 2) + zh
                first = pl.multiple_of((from_x * 2 + from_y // 2) * rows, 16)
                fetch(source, weight.at[layer, pl.ds(first, rows), :], sems.at[layer])
    if last:
        extra = fetch_extra(ring, 16 * tail, share, proj, None, extra_sem)

    act[...] = act_ref[...]

    def layer_step(layer, carry):
        normed[...] = normalize(act[...]).astype(bf16)
        pltpu.make_async_copy(weight.at[layer], weight.at[layer], sems.at[layer]).wait()
        for start in range(0, width, 256):
            cols = pl.ds(start, min(256, width - start))
            update = jnp.dot(normed[...], weight[layer, :, cols], preferred_element_type=f32)
            act[:, cols] = (act[:, cols].astype(f32) + jax.nn.gelu(update)).astype(bf16)
        return carry

    lax.fori_loop(0, 4, layer_step, 0)
    if last:
        for copy in extra:
            copy.wait()
        pooled = jnp.mean(normalize(act[...]), axis=0, keepdims=True)
        pooled = jnp.broadcast_to(pooled, (8, width)).astype(bf16)
        emb = lax.dot_general(pooled, proj[...], NT, preferred_element_type=f32)
        row_ref[...] = scale_ref[0] * lax.dot_general(
            unit_rows(emb), units_ref[...], NT, preferred_element_type=f32
        )


def tower(act, pieces, ring, place, head, tail, share, scale=None, units=None):
    tokens, width = act.shape
    last = units is not None
    vmem, anywhere = pl.BlockSpec(memory_space=pltpu.VMEM), pl.BlockSpec(memory_space=pl.ANY)
    smem = pl.BlockSpec(memory_space=pltpu.SMEM)
    scratch = [
        pltpu.VMEM((4, width, width), bf16),
        pltpu.VMEM((tokens, width), bf16),
        pltpu.SemaphoreType.DMA((4,)),
    ]
    if last:
        out_shape = jax.ShapeDtypeStruct((8, units.shape[0]), f32)
        scratch = [pltpu.VMEM((tokens, width), bf16)] + scratch
        scratch += [pltpu.VMEM((256 * share, width), bf16), pltpu.SemaphoreType.DMA]
        more, more_specs = (scale, units), [smem, vmem]
    else:
        out_shape = jax.ShapeDtypeStruct((tokens, width), bf16)
        more, more_specs = (), []
    return pl.pallas_call(
        functools.partial(tower_kernel, head, tail, share, last),
        out_shape=out_shape,
        in_specs=[smem, vmem] + [anywhere] * 17 + more_specs,
        out_specs=vmem,
        scratch_shapes=scratch,
        compiler_params=pltpu.CompilerParams(vmem_limit_bytes=40 * 1024 * 1024),
        cost_estimate=pl.CostEstimate(
            flops=8 * tokens * width * width, bytes_accessed=8 * width * width, transcendentals=0
        ),
    )(place, act, *pieces, ring, *more)


def hop(value, axis):
    return lax.ppermute(
        value, (axis, "c"),
        [(i * 2 + c, (i + 1 - 2 * c) % 4 * 2 + c) for i in range(4) for c in range(2)],
    )


def gather_plane(block, axis_one, axis_two):
    line = [block]
    for _ in range(3):
        line.append(hop(line[-1], axis_one))
    pairs = []
    for pair in (jnp.stack(line[:2]), jnp.stack(line[2:])):
        pairs.append(pair)
        for _ in range(3):
            pair = hop(pair, axis_two)
            pairs.append(pair)
    return pairs


def on_device(images, text_pooled, image_weight, proj_image, proj_text, logit_scale, pairing):
    y, zh, zl, x, c = (lax.axis_index(name) for name in AXES)
    rows = image_weight.shape[1]
    width, text_width = proj_image.shape[0], proj_text.shape[0]
    micro = images.shape[0]
    head = 22
    tail = rows - head
    share = proj_image.shape[1] // 4
    section = y * 2 + zh
    within = section % 4
    at_home = (y // 2) == c

    order = feature_order(rows, head)

    def ordered(values):
        return jnp.dot(values, order, preferred_element_type=f32).astype(bf16)

    crossing = [(p * 2 + 1, (p + 2) * 2) for p in (0, 1)] + [(p * 2, (p - 2) * 2 + 1) for p in (2, 3)]
    weight = image_weight[0]
    weight = ordered(jnp.where(at_home, weight, lax.ppermute(weight, ("y", "c"), crossing)))

    def share_of(projection):
        return lax.dynamic_slice_in_dim(projection, within * share, share, 1).T

    text_row = lax.dynamic_slice_in_dim(text_pooled, within, 1, 0)
    widen = ((0, 0), (0, width - text_width))
    text_rows = jnp.pad(jnp.concatenate([share_of(proj_text), text_row]), widen)
    image_rows = jnp.pad(ordered(share_of(proj_image)), ((0, 1), (0, 0)))
    first_core = c == 0
    extra = jnp.where(
        at_home,
        jnp.where(first_core, text_rows, image_rows),
        swap(jnp.where(first_core, image_rows, text_rows)),
    )
    image = ordered(lax.dynamic_index_in_dim(images, within, 0, False))
    image = jnp.where(at_home, image, swap(image))

    column = lax.all_gather(weight[:head], Z, axis=0).reshape(2, 8 * head, width)
    small = jnp.concatenate([weight[head:], extra])
    spread = lax.all_to_all(
        jnp.broadcast_to(small[None], (16,) + small.shape), ("y", "x"), 0, 0, tiled=True
    )
    weight_part = spread[:, :tail].reshape(2, 2, 4, tail, width).transpose(1, 0, 2, 3, 4)
    plane_rows = jnp.concatenate([
        weight_part.reshape(16 * tail, width),
        spread[:, tail:tail + share].reshape(16 * share, width),
        spread[:, tail + share],
    ])
    ring = lax.all_gather(plane_rows, Z, axis=0)
    pieces = gather_plane(column[0], "x", "y") + gather_plane(column[1], "y", "x")

    units = swap(text_units(ring, 16 * tail, share, 256, text_width))
    place = jnp.stack([x, y, 2 * c - 1]).astype(jnp.int32)
    act = tower(image, pieces, ring, place, head, tail, share)
    row = tower(swap(act), pieces, ring, place, head, tail, share, logit_scale, units)[:1]
    row = jnp.where(first_core, swap(row), row)

    count = row.shape[1]
    rows_of_z = lax.all_to_all(jnp.broadcast_to(row[None], (16, 1, count)), Z, 0, 0, tiled=True)
    logits = lax.all_to_all(
        jnp.broadcast_to(rows_of_z.reshape(1, 16, count), (16, 16, count)), ("y", "x"), 0, 0, tiled=True
    )
    by_chip = logits.reshape(2, 2, 4, 2, 8, count)
    zero = jnp.int32(0)
    own_logits = lax.dynamic_slice(
        by_chip, (c, zero, x, zero, zl, zero), (1, 2, 1, 2, 1, count)
    ).reshape(micro, count)
    row_start = ((zl * 4 + x) * 2 + c) * micro
    column_lse = jnp.log(jnp.sum(jnp.exp(logits.reshape(256, count)), axis=0))
    own_pairs = lax.dynamic_slice_in_dim(pairing, row_start, micro, 0)
    paired = own_pairs[:, None] == lax.broadcasted_iota(jnp.int32, (1, count), 1)
    positive = jnp.sum(jnp.where(paired, own_logits, 0.0), axis=1)
    image_loss = jnp.log(jnp.sum(jnp.exp(own_logits), axis=1)) - positive
    text_loss = jnp.sum(jnp.where(paired, column_lse[None, :], 0.0), axis=1) - positive
    columns = count // 8
    logit_block = lax.dynamic_slice_in_dim(own_logits, section * columns, columns, 1)
    return (logit_block, image_loss, text_loss)


def solution(mesh):
    fine = Mesh(mesh.devices.reshape(SIZES), AXES)
    section, dp = ("y", "zh"), ("zl", "x", "c")
    in_specs = (
        P(dp, None, None),
        P(dp, None),
        P(section, dp, None),
        P(None, dp),
        P(None, dp),
        P(),
        P(),
    )
    out_specs = (P(dp, section), P(dp), P(dp))
    return jax.shard_map(on_device, mesh=fine, in_specs=in_specs, out_specs=out_specs, check_vma=False)
```

```python
import functools

import jax
import jax.numpy as jnp
from jax import lax
from jax.experimental import pallas as pl
from jax.experimental.pallas import tpu as pltpu
from jax.sharding import Mesh, PartitionSpec as P

AXES = ("y", "zh", "zl", "x", "c")
SIZES = (4, 2, 8, 4, 2)
CHIPS = ("y", "zh", "zl", "x")
Z = ("zh", "zl")
bf16, f32 = jnp.bfloat16, jnp.float32


def swap(value):
    return lax.ppermute(value, "c", [(0, 1), (1, 0)])


def normalize(values):
    values = values.astype(f32)
    center = jnp.mean(values, axis=-1, keepdims=True)
    spread = jnp.mean((values - center) ** 2, axis=-1, keepdims=True)
    return (values - center) / jnp.sqrt(spread + 1e-05)


def feature_order(rows, head):
    width = rows * 64
    tail = rows - head
    natural = lax.broadcasted_iota(jnp.int32, (width, 1), 0)
    row = natural % rows
    core = (natural // rows) % 2
    x = (natural // (rows * 2)) % 4
    zl = natural // (rows * 8)
    first = (x * 2 + core) * (8 * head) + zl * head + row
    second = 64 * head + zl * (8 * tail) + (core * 4 + x) * tail + row - head
    place = jnp.where(row < head, first, second)
    return (place == lax.broadcasted_iota(jnp.int32, (1, width), 1)).astype(bf16)


def fetch(source, target, sem):
    copy = pltpu.make_async_copy(source, target, sem)
    copy.start()
    return copy


def fetch_extra(ring_ref, first, share, proj, texts, sem):
    copies = []
    for z in range(16):
        rows = 16 * share
        copies.append(fetch(ring_ref.at[z, pl.ds(first, rows), :], proj.at[pl.ds(z * rows, rows), :], sem))
        if texts is not None:
            copies.append(fetch(
                ring_ref.at[z, pl.ds(first + rows, 16), :], texts.at[pl.ds(z * 16, 16), :], sem
            ))
    return copies


NT = (((1,), (1,)), ((), ()))


def unit_rows(emb):
    square = jnp.sum(emb * emb, axis=1, keepdims=True)
    return (emb / jnp.sqrt(square + 1e-06)).astype(bf16)


def texts_kernel(first, share, ring_ref, out_ref, proj, texts, sem):
    for copy in fetch_extra(ring_ref, first, share, proj, texts, sem):
        copy.wait()
    count, width = out_ref.shape
    emb = lax.dot_general(texts[:, :width], proj[:, :width], NT, preferred_element_type=f32)
    held = lax.broadcasted_iota(jnp.int32, (count, count), 1)
    zh, zl, y, x = held >> 7, (held >> 4) & 7, (held >> 2) & 3, held & 3
    index = zl * 32 + x * 8 + (y >> 1) * 4 + (y & 1) * 2 + zh
    order = (index == lax.broadcasted_iota(jnp.int32, (count, count), 0)).astype(bf16)
    out_ref[...] = jnp.dot(order, unit_rows(emb), preferred_element_type=f32).astype(bf16)


def text_units(ring, first, share, count, text_width):
    width = ring.shape[2]
    return pl.pallas_call(
        functools.partial(texts_kernel, first, share),
        out_shape=jax.ShapeDtypeStruct((count, text_width), bf16),
        in_specs=[pl.BlockSpec(memory_space=pl.ANY)],
        out_specs=pl.BlockSpec(memory_space=pltpu.VMEM),
        scratch_shapes=[
            pltpu.VMEM((256 * share, width), bf16),
            pltpu.VMEM((count, width), bf16),
            pltpu.SemaphoreType.DMA,
        ],
        compiler_params=pltpu.CompilerParams(vmem_limit_bytes=32 * 1024 * 1024),
        cost_estimate=pl.CostEstimate(
            flops=2 * count * text_width * text_width,
            bytes_accessed=512 * share * width, transcendentals=0,
        ),
    )(ring)


def tower_kernel(head, tail, share, last, place_ref, act_ref, *refs):
    pieces, ring, refs = refs[:16], refs[16], refs[17:]
    if last:
        scale_ref, units_ref, row_ref, act, weight, normed, sems, proj, extra_sem = refs
    else:
        act, weight, normed, sems = refs
    x, y, sign = place_ref[0], place_ref[1], place_ref[2]
    rows = 8 * head
    width = act_ref.shape[1]

    for zh in range(2):
        for pair in range(2):
            layer = 2 * pair + zh
            for zl in range(8):
                fetch(
                    ring.at[zh * 8 + zl, pl.ds(pair * 8 * tail, 8 * tail), :],
                    weight.at[layer, pl.ds(8 * rows + zl * 8 * tail, 8 * tail), :],
                    sems.at[layer],
                )
        for inner in range(4):
            for outer in range(4):
                source = pieces[zh * 8 + (inner // 2) * 4 + outer].at[inner % 2]
                by_x, by_y = (inner, outer) if zh == 0 else (outer, inner)
                from_x, from_y = (x + 4 + sign * by_x) % 4, (y + 4 + sign * by_y) % 4
                layer = 2 * (from_y % 2) + zh
                first = pl.multiple_of((from_x * 2 + from_y // 2) * rows, 16)
                fetch(source, weight.at[layer, pl.ds(first, rows), :], sems.at[layer])
    if last:
        extra = fetch_extra(ring, 16 * tail, share, proj, None, extra_sem)

    act[...] = act_ref[...]

    def layer_step(layer, carry):
        normed[...] = normalize(act[...]).astype(bf16)
        pltpu.make_async_copy(weight.at[layer], weight.at[layer], sems.at[layer]).wait()
        for start in range(0, width, 256):
            cols = pl.ds(start, min(256, width - start))
            update = jnp.dot(normed[...], weight[layer, :, cols], preferred_element_type=f32)
            act[:, cols] = (act[:, cols].astype(f32) + jax.nn.gelu(update)).astype(bf16)
        return carry

    lax.fori_loop(0, 4, layer_step, 0)
    if last:
        for copy in extra:
            copy.wait()
        pooled = jnp.mean(normalize(act[...]), axis=0, keepdims=True)
        pooled = jnp.broadcast_to(pooled, (8, width)).astype(bf16)
        emb = lax.dot_general(pooled, proj[...], NT, preferred_element_type=f32)
        row_ref[...] = scale_ref[0] * lax.dot_general(
            unit_rows(emb), units_ref[...], NT, preferred_element_type=f32
        )


def tower(act, pieces, ring, place, head, tail, share, scale=None, units=None):
    tokens, width = act.shape
    last = units is not None
    vmem, anywhere = pl.BlockSpec(memory_space=pltpu.VMEM), pl.BlockSpec(memory_space=pl.ANY)
    smem = pl.BlockSpec(memory_space=pltpu.SMEM)
    scratch = [
        pltpu.VMEM((4, width, width), bf16),
        pltpu.VMEM((tokens, width), bf16),
        pltpu.SemaphoreType.DMA((4,)),
    ]
    if last:
        out_shape = jax.ShapeDtypeStruct((8, units.shape[0]), f32)
        scratch = [pltpu.VMEM((tokens, width), bf16)] + scratch
        scratch += [pltpu.VMEM((256 * share, width), bf16), pltpu.SemaphoreType.DMA]
        more, more_specs = (scale, units), [smem, vmem]
    else:
        out_shape = jax.ShapeDtypeStruct((tokens, width), bf16)
        more, more_specs = (), []
    return pl.pallas_call(
        functools.partial(tower_kernel, head, tail, share, last),
        out_shape=out_shape,
        in_specs=[smem, vmem] + [anywhere] * 17 + more_specs,
        out_specs=vmem,
        scratch_shapes=scratch,
        compiler_params=pltpu.CompilerParams(vmem_limit_bytes=40 * 1024 * 1024),
        cost_estimate=pl.CostEstimate(
            flops=8 * tokens * width * width, bytes_accessed=8 * width * width, transcendentals=0
        ),
    )(place, act, *pieces, ring, *more)


def hop(value, axis):
    return lax.ppermute(
        value, (axis, "c"),
        [(i * 2 + c, (i + 1 - 2 * c) % 4 * 2 + c) for i in range(4) for c in range(2)],
    )


def gather_plane(block_one, block_two):
    axes = (("x", "y"), ("y", "x"))
    start = [block_one, block_two]
    first = [hop(start[i], axes[i][0]) for i in range(2)]
    near = [jnp.stack([start[i], first[i]]) for i in range(2)]
    second = [hop(first[i], axes[i][0]) for i in range(2)]
    near_one = [hop(near[i], axes[i][1]) for i in range(2)]
    second, near_one = lax.optimization_barrier((second, near_one))
    third = [hop(second[i], axes[i][0]) for i in range(2)]
    near_two = [hop(near_one[i], axes[i][1]) for i in range(2)]
    third, near_two = lax.optimization_barrier((third, near_two))
    far = [jnp.stack([second[i], third[i]]) for i in range(2)]
    far_one = [hop(far[i], axes[i][1]) for i in range(2)]
    near_three = [hop(near_two[i], axes[i][1]) for i in range(2)]
    far_two = [hop(far_one[i], axes[i][1]) for i in range(2)]
    far_three = [hop(far_two[i], axes[i][1]) for i in range(2)]
    pairs = []
    for i in range(2):
        pairs += [near[i], near_one[i], near_two[i], near_three[i]]
        pairs += [far[i], far_one[i], far_two[i], far_three[i]]
    return pairs


def ahead_on_ring(value, steps):
    return lax.ppermute(value, Z, [((i + steps) % 16, i) for i in range(16)])


def gather_ring(block, position):
    near = {0: block}
    for ahead in (8, 4, 12):
        near[ahead] = ahead_on_ring(block, ahead)
    stack = jnp.stack([near[ahead] for ahead in (0, 4, 8, 12)])
    one, three = ahead_on_ring(stack, 1), ahead_on_ring(stack, -1)
    two_a = ahead_on_ring(jnp.stack([near[0], near[4]]), 2)
    two_b = ahead_on_ring(jnp.stack([near[0], near[12]]), -2)
    blocks = {2: two_a[0], 6: two_a[1], 14: two_b[0], 10: two_b[1]}
    for k in range(4):
        blocks[4 * k] = stack[k]
        blocks[4 * k + 1] = one[k]
        blocks[(4 * k + 15) % 16] = three[k]
    line = jnp.stack([blocks[k % 16] for k in range(32)])
    return lax.dynamic_slice_in_dim(line, (16 - position) % 16, 16, 0)


def on_device(images, text_pooled, image_weight, proj_image, proj_text, logit_scale, pairing):
    y, zh, zl, x, c = (lax.axis_index(name) for name in AXES)
    rows = image_weight.shape[1]
    width, text_width = proj_image.shape[0], proj_text.shape[0]
    micro = images.shape[0]
    head = 22
    tail = rows - head
    share = proj_image.shape[1] // 4
    section = y * 2 + zh
    within = section % 4
    at_home = (y // 2) == c

    order = feature_order(rows, head)

    def ordered(values):
        return jnp.dot(values, order, preferred_element_type=f32).astype(bf16)

    crossing = [(p * 2 + 1, (p + 2) * 2) for p in (0, 1)] + [(p * 2, (p - 2) * 2 + 1) for p in (2, 3)]
    weight = image_weight[0]
    weight = ordered(jnp.where(at_home, weight, lax.ppermute(weight, ("y", "c"), crossing)))

    def share_of(projection):
        return lax.dynamic_slice_in_dim(projection, within * share, share, 1).T

    text_row = lax.dynamic_slice_in_dim(text_pooled, within, 1, 0)
    widen = ((0, 0), (0, width - text_width))
    text_rows = jnp.pad(jnp.concatenate([share_of(proj_text), text_row]), widen)
    image_rows = jnp.pad(ordered(share_of(proj_image)), ((0, 1), (0, 0)))
    first_core = c == 0
    extra = jnp.where(
        at_home,
        jnp.where(first_core, text_rows, image_rows),
        swap(jnp.where(first_core, image_rows, text_rows)),
    )
    image = ordered(lax.dynamic_index_in_dim(images, within, 0, False))
    image = jnp.where(at_home, image, swap(image))

    small = jnp.concatenate([weight[head:], extra])
    small, block = lax.optimization_barrier((small, weight[:head]))
    spread = lax.all_gather(small, ("y", "x"), axis=0)
    column = gather_ring(block, zh * 8 + zl).reshape(2, 8 * head, width)
    weight_part = spread[:, :tail].reshape(2, 2, 4, tail, width).transpose(1, 0, 2, 3, 4)
    plane_rows = jnp.concatenate([
        weight_part.reshape(16 * tail, width),
        spread[:, tail:tail + share].reshape(16 * share, width),
        spread[:, tail + share],
    ])
    ring = lax.all_gather(plane_rows, Z, axis=0)
    pieces = gather_plane(column[0], column[1])

    units = swap(text_units(ring, 16 * tail, share, 256, text_width))
    place = jnp.stack([x, y, 2 * c - 1]).astype(jnp.int32)
    act = tower(image, pieces, ring, place, head, tail, share)
    row = tower(swap(act), pieces, ring, place, head, tail, share, logit_scale, units)[:1]
    row = jnp.where(first_core, swap(row), row)

    count = row.shape[1]
    rows_of_z = lax.all_to_all(jnp.broadcast_to(row[None], (16, 1, count)), Z, 0, 0, tiled=True)
    logits = lax.all_to_all(
        jnp.broadcast_to(rows_of_z.reshape(1, 16, count), (16, 16, count)), ("y", "x"), 0, 0, tiled=True
    )
    by_chip = logits.reshape(2, 2, 4, 2, 8, count)
    zero = jnp.int32(0)
    own_logits = lax.dynamic_slice(
        by_chip, (c, zero, x, zero, zl, zero), (1, 2, 1, 2, 1, count)
    ).reshape(micro, count)
    row_start = ((zl * 4 + x) * 2 + c) * micro
    column_lse = jnp.log(jnp.sum(jnp.exp(logits.reshape(256, count)), axis=0))
    own_pairs = lax.dynamic_slice_in_dim(pairing, row_start, micro, 0)
    paired = own_pairs[:, None] == lax.broadcasted_iota(jnp.int32, (1, count), 1)
    positive = jnp.sum(jnp.where(paired, own_logits, 0.0), axis=1)
    image_loss = jnp.log(jnp.sum(jnp.exp(own_logits), axis=1)) - positive
    text_loss = jnp.sum(jnp.where(paired, column_lse[None, :], 0.0), axis=1) - positive
    columns = count // 8
    logit_block = lax.dynamic_slice_in_dim(own_logits, section * columns, columns, 1)
    return (logit_block, image_loss, text_loss)


def solution(mesh):
    fine = Mesh(mesh.devices.reshape(SIZES), AXES)
    section, dp = ("y", "zh"), ("zl", "x", "c")
    in_specs = (
        P(dp, None, None),
        P(dp, None),
        P(section, dp, None),
        P(None, dp),
        P(None, dp),
        P(),
        P(),
    )
    out_specs = (P(dp, section), P(dp), P(dp))
    return jax.shard_map(on_device, mesh=fine, in_specs=in_specs, out_specs=out_specs, check_vma=False)
```

```python
import functools

import jax
import jax.numpy as jnp
from jax import lax
from jax.experimental import pallas as pl
from jax.experimental.pallas import tpu as pltpu
from jax.sharding import Mesh, PartitionSpec as P

AXES = ("y", "zh", "zl", "x", "c")
SIZES = (4, 2, 8, 4, 2)
CHIPS = ("y", "zh", "zl", "x")
Z = ("zh", "zl")
bf16, f32 = jnp.bfloat16, jnp.float32


def swap(value):
    return lax.ppermute(value, "c", [(0, 1), (1, 0)])


def normalize(values):
    values = values.astype(f32)
    center = jnp.mean(values, axis=-1, keepdims=True)
    spread = jnp.mean((values - center) ** 2, axis=-1, keepdims=True)
    return (values - center) / jnp.sqrt(spread + 1e-05)


def feature_order(rows, head):
    width = rows * 64
    tail = rows - head
    natural = lax.broadcasted_iota(jnp.int32, (width, 1), 0)
    row = natural % rows
    core = (natural // rows) % 2
    x = (natural // (rows * 2)) % 4
    zl = natural // (rows * 8)
    first = (x * 2 + core) * (8 * head) + zl * head + row
    second = 64 * head + zl * (8 * tail) + (core * 4 + x) * tail + row - head
    place = jnp.where(row < head, first, second)
    return (place == lax.broadcasted_iota(jnp.int32, (1, width), 1)).astype(bf16)


def fetch(source, target, sem):
    copy = pltpu.make_async_copy(source, target, sem)
    copy.start()
    return copy


def fetch_extra(ring_ref, first, share, proj, texts, sem):
    copies = []
    for z in range(16):
        rows = 16 * share
        copies.append(fetch(ring_ref.at[z, pl.ds(first, rows), :], proj.at[pl.ds(z * rows, rows), :], sem))
        if texts is not None:
            copies.append(fetch(
                ring_ref.at[z, pl.ds(first + rows, 16), :], texts.at[pl.ds(z * 16, 16), :], sem
            ))
    return copies


NT = (((1,), (1,)), ((), ()))


def unit_rows(emb):
    square = jnp.sum(emb * emb, axis=1, keepdims=True)
    return (emb / jnp.sqrt(square + 1e-06)).astype(bf16)


def texts_kernel(first, share, ring_ref, out_ref, proj, texts, sem):
    for copy in fetch_extra(ring_ref, first, share, proj, texts, sem):
        copy.wait()
    count, width = out_ref.shape
    emb = lax.dot_general(texts[:, :width], proj[:, :width], NT, preferred_element_type=f32)
    held = lax.broadcasted_iota(jnp.int32, (count, count), 1)
    zh, zl, y, x = held >> 7, (held >> 4) & 7, (held >> 2) & 3, held & 3
    index = zl * 32 + x * 8 + (y >> 1) * 4 + (y & 1) * 2 + zh
    order = (index == lax.broadcasted_iota(jnp.int32, (count, count), 0)).astype(bf16)
    out_ref[...] = jnp.dot(order, unit_rows(emb), preferred_element_type=f32).astype(bf16)


def text_units(ring, first, share, count, text_width):
    width = ring.shape[2]
    return pl.pallas_call(
        functools.partial(texts_kernel, first, share),
        out_shape=jax.ShapeDtypeStruct((count, text_width), bf16),
        in_specs=[pl.BlockSpec(memory_space=pl.ANY)],
        out_specs=pl.BlockSpec(memory_space=pltpu.VMEM),
        scratch_shapes=[
            pltpu.VMEM((256 * share, width), bf16),
            pltpu.VMEM((count, width), bf16),
            pltpu.SemaphoreType.DMA,
        ],
        compiler_params=pltpu.CompilerParams(vmem_limit_bytes=32 * 1024 * 1024),
        cost_estimate=pl.CostEstimate(
            flops=2 * count * text_width * text_width,
            bytes_accessed=512 * share * width, transcendentals=0,
        ),
    )(ring)


def tower_kernel(head, tail, share, last, place_ref, act_ref, *refs):
    pieces, ring, refs = refs[:24], refs[24], refs[25:]
    if last:
        scale_ref, units_ref, row_ref, act, weight, normed, sems, proj, extra_sem = refs
    else:
        act, weight, normed, sems = refs
    x, y, sign = place_ref[0], place_ref[1], place_ref[2]
    rows = 8 * head
    width = act_ref.shape[1]

    for zh in range(2):
        for pair in range(2):
            layer = 2 * pair + zh
            for zl in range(8):
                fetch(
                    ring.at[zh * 8 + zl, pl.ds(pair * 8 * tail, 8 * tail), :],
                    weight.at[layer, pl.ds(8 * rows + zl * 8 * tail, 8 * tail), :],
                    sems.at[layer],
                )
        for inner in range(4):
            for outer in range(4):
                source = pieces[zh * 12 + min(inner, 2) * 4 + outer]
                source = source if inner < 2 else source.at[inner - 2]
                by_x, by_y = (inner, outer) if zh == 0 else (outer, inner)
                from_x, from_y = (x + 4 + sign * by_x) % 4, (y + 4 + sign * by_y) % 4
                layer = 2 * (from_y % 2) + zh
                first = pl.multiple_of((from_x * 2 + from_y // 2) * rows, 16)
                fetch(source, weight.at[layer, pl.ds(first, rows), :], sems.at[layer])
    if last:
        extra = fetch_extra(ring, 16 * tail, share, proj, None, extra_sem)

    act[...] = act_ref[...]

    def layer_step(layer, carry):
        normed[...] = normalize(act[...]).astype(bf16)
        pltpu.make_async_copy(weight.at[layer], weight.at[layer], sems.at[layer]).wait()
        for start in range(0, width, 256):
            cols = pl.ds(start, min(256, width - start))
            update = jnp.dot(normed[...], weight[layer, :, cols], preferred_element_type=f32)
            act[:, cols] = (act[:, cols].astype(f32) + jax.nn.gelu(update)).astype(bf16)
        return carry

    lax.fori_loop(0, 4, layer_step, 0)
    if last:
        for copy in extra:
            copy.wait()
        pooled = jnp.mean(normalize(act[...]), axis=0, keepdims=True)
        pooled = jnp.broadcast_to(pooled, (8, width)).astype(bf16)
        emb = lax.dot_general(pooled, proj[...], NT, preferred_element_type=f32)
        row_ref[...] = scale_ref[0] * lax.dot_general(
            unit_rows(emb), units_ref[...], NT, preferred_element_type=f32
        )


def tower(act, pieces, ring, place, head, tail, share, scale=None, units=None):
    tokens, width = act.shape
    last = units is not None
    vmem, anywhere = pl.BlockSpec(memory_space=pltpu.VMEM), pl.BlockSpec(memory_space=pl.ANY)
    smem = pl.BlockSpec(memory_space=pltpu.SMEM)
    scratch = [
        pltpu.VMEM((4, width, width), bf16),
        pltpu.VMEM((tokens, width), bf16),
        pltpu.SemaphoreType.DMA((4,)),
    ]
    if last:
        out_shape = jax.ShapeDtypeStruct((8, units.shape[0]), f32)
        scratch = [pltpu.VMEM((tokens, width), bf16)] + scratch
        scratch += [pltpu.VMEM((256 * share, width), bf16), pltpu.SemaphoreType.DMA]
        more, more_specs = (scale, units), [smem, vmem]
    else:
        out_shape = jax.ShapeDtypeStruct((tokens, width), bf16)
        more, more_specs = (), []
    return pl.pallas_call(
        functools.partial(tower_kernel, head, tail, share, last),
        out_shape=out_shape,
        in_specs=[smem, vmem] + [anywhere] * 25 + more_specs,
        out_specs=vmem,
        scratch_shapes=scratch,
        compiler_params=pltpu.CompilerParams(vmem_limit_bytes=40 * 1024 * 1024),
        cost_estimate=pl.CostEstimate(
            flops=8 * tokens * width * width, bytes_accessed=8 * width * width, transcendentals=0
        ),
    )(place, act, *pieces, ring, *more)


def hop(value, axis):
    return lax.ppermute(
        value, (axis, "c"),
        [(i * 2 + c, (i + 1 - 2 * c) % 4 * 2 + c) for i in range(4) for c in range(2)],
    )


def gather_plane(block_one, block_two):
    pieces = []
    for block, axis_one, axis_two in ((block_one, "x", "y"), (block_two, "y", "x")):
        own = [block, hop(block, axis_two)]
        one, own[1] = lax.optimization_barrier((hop(block, axis_one), own[1]))
        near = [one, hop(one, axis_two)]
        two, near[1] = lax.optimization_barrier((hop(one, axis_one), near[1]))
        pair = [jnp.stack([two, hop(two, axis_one)])]
        for chain in (own, near, pair):
            while len(chain) < 4:
                chain.append(hop(chain[-1], axis_two))
            pieces += chain
    return pieces


def ahead_on_ring(value, steps):
    return lax.ppermute(value, Z, [((i + steps) % 16, i) for i in range(16)])


def line_kernel(position_ref, stack, one, two_a, two_b, three, out_ref):
    for k in range(4):
        blocks = (
            (4 * k, stack[k]), (4 * k + 1, one[k]), (4 * k + 15, three[k]),
            ((2, 6)[k] if k < 2 else (14, 10)[k - 2], two_a[k] if k < 2 else two_b[k - 2]),
        )
        for ahead, block in blocks:
            out_ref[(position_ref[0] + ahead) % 16] = block


def gather_ring(block, position):
    near = {0: block}
    for ahead in (8, 4, 12):
        near[ahead] = ahead_on_ring(block, ahead)
    stack = jnp.stack([near[ahead] for ahead in (0, 4, 8, 12)])
    one, three = ahead_on_ring(stack, 1), ahead_on_ring(stack, -1)
    two_a = ahead_on_ring(stack[:2], 2)
    two_b = ahead_on_ring(jnp.stack([near[0], near[12]]), -2)
    vmem = pl.BlockSpec(memory_space=pltpu.VMEM)
    return pl.pallas_call(
        line_kernel,
        out_shape=jax.ShapeDtypeStruct((16,) + block.shape, block.dtype),
        in_specs=[pl.BlockSpec(memory_space=pltpu.SMEM)] + [vmem] * 5,
        out_specs=vmem,
        compiler_params=pltpu.CompilerParams(vmem_limit_bytes=16 * 1024 * 1024),
    )(position[None], stack, one, two_a, two_b, three)


def on_device(images, text_pooled, image_weight, proj_image, proj_text, logit_scale, pairing):
    y, zh, zl, x, c = (lax.axis_index(name) for name in AXES)
    rows = image_weight.shape[1]
    width, text_width = proj_image.shape[0], proj_text.shape[0]
    micro = images.shape[0]
    head = 22
    tail = rows - head
    share = proj_image.shape[1] // 4
    section = y * 2 + zh
    within = section % 4
    at_home = (y // 2) == c

    order = feature_order(rows, head)

    def ordered(values):
        return jnp.dot(values, order, preferred_element_type=f32).astype(bf16)

    crossing = [(p * 2 + 1, (p + 2) * 2) for p in (0, 1)] + [(p * 2, (p - 2) * 2 + 1) for p in (2, 3)]
    weight = image_weight[0]
    weight = ordered(jnp.where(at_home, weight, lax.ppermute(weight, ("y", "c"), crossing)))

    def share_of(projection):
        return lax.dynamic_slice_in_dim(projection, within * share, share, 1).T

    text_row = lax.dynamic_slice_in_dim(text_pooled, within, 1, 0)
    widen = ((0, 0), (0, width - text_width))
    text_rows = jnp.pad(jnp.concatenate([share_of(proj_text), text_row]), widen)
    image_rows = jnp.pad(ordered(share_of(proj_image)), ((0, 1), (0, 0)))
    first_core = c == 0
    extra = jnp.where(
        at_home,
        jnp.where(first_core, text_rows, image_rows),
        swap(jnp.where(first_core, image_rows, text_rows)),
    )
    image = ordered(lax.dynamic_index_in_dim(images, within, 0, False))
    image = jnp.where(at_home, image, swap(image))

    small = jnp.concatenate([weight[head:], extra])
    small = jnp.pad(small, ((0, 24 - small.shape[0]), (0, 0)))
    small, block = lax.optimization_barrier((small, weight[:head]))
    spread = lax.all_gather(small, ("y", "x"), axis=0)
    column = gather_ring(block, zh * 8 + zl).reshape(2, 8 * head, width)
    weight_part = spread[:, :tail].reshape(2, 2, 4, tail, width).transpose(1, 0, 2, 3, 4)
    plane_rows = jnp.concatenate([
        weight_part.reshape(16 * tail, width),
        spread[:, tail:tail + share].reshape(16 * share, width),
        spread[:, tail + share],
    ])
    plane_rows, column = lax.optimization_barrier((plane_rows, column))
    ring = lax.all_gather(plane_rows, Z, axis=0)
    pieces = gather_plane(column[0], column[1])

    units = swap(text_units(ring, 16 * tail, share, 256, text_width))
    place = jnp.stack([x, y, 2 * c - 1]).astype(jnp.int32)
    act = tower(image, pieces, ring, place, head, tail, share)
    row = tower(swap(act), pieces, ring, place, head, tail, share, logit_scale, units)[:1]
    row = jnp.where(first_core, swap(row), row)

    count = row.shape[1]
    rows_of_z = lax.all_to_all(jnp.broadcast_to(row[None], (16, 1, count)), Z, 0, 0, tiled=True)
    logits = lax.all_to_all(
        jnp.broadcast_to(rows_of_z.reshape(1, 16, count), (16, 16, count)), ("y", "x"), 0, 0, tiled=True
    )
    by_chip = logits.reshape(2, 2, 4, 2, 8, count)
    zero = jnp.int32(0)
    own_logits = lax.dynamic_slice(
        by_chip, (c, zero, x, zero, zl, zero), (1, 2, 1, 2, 1, count)
    ).reshape(micro, count)
    row_start = ((zl * 4 + x) * 2 + c) * micro
    column_lse = jnp.log(jnp.sum(jnp.exp(logits.reshape(256, count)), axis=0))
    own_pairs = lax.dynamic_slice_in_dim(pairing, row_start, micro, 0)
    paired = own_pairs[:, None] == lax.broadcasted_iota(jnp.int32, (1, count), 1)
    positive = jnp.sum(jnp.where(paired, own_logits, 0.0), axis=1)
    image_loss = jnp.log(jnp.sum(jnp.exp(own_logits), axis=1)) - positive
    text_loss = jnp.sum(jnp.where(paired, column_lse[None, :], 0.0), axis=1) - positive
    columns = count // 8
    logit_block = lax.dynamic_slice_in_dim(own_logits, section * columns, columns, 1)
    return (logit_block, image_loss, text_loss)


def solution(mesh):
    fine = Mesh(mesh.devices.reshape(SIZES), AXES)
    section, dp = ("y", "zh"), ("zl", "x", "c")
    in_specs = (
        P(dp, None, None),
        P(dp, None),
        P(section, dp, None),
        P(None, dp),
        P(None, dp),
        P(),
        P(),
    )
    out_specs = (P(dp, section), P(dp), P(dp))
    return jax.shard_map(on_device, mesh=fine, in_specs=in_specs, out_specs=out_specs, check_vma=False)
```

```python
import functools

import jax
import jax.numpy as jnp
from jax import lax
from jax.experimental import pallas as pl
from jax.experimental.pallas import tpu as pltpu
from jax.sharding import Mesh, PartitionSpec as P

AXES = ("y", "zh", "zl", "x", "c")
SIZES = (4, 2, 8, 4, 2)
Z = ("zh", "zl")
NT = (((1,), (1,)), ((), ()))
bf16, f32 = jnp.bfloat16, jnp.float32
VMEM, ANYWHERE = pl.BlockSpec(memory_space=pltpu.VMEM), pl.BlockSpec(memory_space=pl.ANY)
SMEM = pl.BlockSpec(memory_space=pltpu.SMEM)

FIRST, SECOND, FIRST_EXTRA, SECOND_EXTRA, TEXTS, BLOCK = 112, 96, 32, 48, 16, 160


def params(mebibytes):
    return pltpu.CompilerParams(vmem_limit_bytes=mebibytes * 1024 * 1024)


def normalize(values):
    values = values.astype(f32)
    center = jnp.mean(values, axis=-1, keepdims=True)
    spread = jnp.mean((values - center) ** 2, axis=-1, keepdims=True)
    return (values - center) / jnp.sqrt(spread + 1e-05)


def unit_rows(emb):
    square = jnp.sum(emb * emb, axis=1, keepdims=True)
    return (emb / jnp.sqrt(square + 1e-06)).astype(bf16)


def fetch(source, target, sem):
    copy = pltpu.make_async_copy(source, target, sem)
    copy.start()
    return copy


def weights_kernel(ring, weights, sem):
    copies = []
    for z in range(16):
        layer, row = z // 8, z % 8 * (FIRST + SECOND)
        for core, start, count in ((0, row, FIRST), (1, row + FIRST, SECOND)):
            copies.append(fetch(
                ring.at[z, core, pl.ds(0, count), :], weights.at[layer, pl.ds(start, count), :], sem
            ))
    for copy in copies:
        copy.wait()


def layer_weights(ring):
    width = ring.shape[-1]
    return pl.pallas_call(
        weights_kernel,
        out_shape=jax.ShapeDtypeStruct((2, width, width), bf16),
        in_specs=[ANYWHERE],
        out_specs=ANYWHERE,
        scratch_shapes=[pltpu.SemaphoreType.DMA],
        compiler_params=params(47),
        cost_estimate=pl.CostEstimate(flops=0, bytes_accessed=8 * width * width, transcendentals=0),
    )(ring)


def texts_kernel(ring, units_ref, proj, texts, sem):
    copies = []
    for z in range(16):
        row = z * (FIRST_EXTRA + SECOND_EXTRA)
        for core, source, target, count in (
            (0, FIRST, row, FIRST_EXTRA), (1, SECOND, row + FIRST_EXTRA, SECOND_EXTRA)
        ):
            copies.append(fetch(
                ring.at[z, core, pl.ds(source, count), :], proj.at[pl.ds(target, count), :], sem
            ))
        copies.append(fetch(
            ring.at[z, 0, pl.ds(FIRST + FIRST_EXTRA, TEXTS), :], texts.at[pl.ds(z * TEXTS, TEXTS), :], sem
        ))
    for copy in copies:
        copy.wait()
    count, width = units_ref.shape
    emb = lax.dot_general(texts[:, :width], proj[:, :width], NT, preferred_element_type=f32)
    held = lax.broadcasted_iota(jnp.int32, (count, count), 1)
    index = ((held >> 1) & 63) * 4 + (held >> 7) * 2 + (held & 1)
    order = (index == lax.broadcasted_iota(jnp.int32, (count, count), 0)).astype(bf16)
    units_ref[...] = jnp.dot(order, unit_rows(emb), preferred_element_type=f32).astype(bf16)


def projection_and_texts(ring, count, text_width):
    width = ring.shape[-1]
    rows = 16 * (FIRST_EXTRA + SECOND_EXTRA)
    return pl.pallas_call(
        texts_kernel,
        out_shape=(
            jax.ShapeDtypeStruct((count, text_width), bf16),
            jax.ShapeDtypeStruct((rows, width), bf16),
        ),
        in_specs=[ANYWHERE],
        out_specs=(VMEM, VMEM),
        scratch_shapes=[pltpu.VMEM((16 * TEXTS, width), bf16), pltpu.SemaphoreType.DMA],
        compiler_params=params(47),
        cost_estimate=pl.CostEstimate(
            flops=2 * count * text_width * rows, bytes_accessed=2 * rows * width, transcendentals=0
        ),
    )(ring)


def layers_kernel(act_ref, weights, out_ref, normed):
    width = act_ref.shape[1]
    out_ref[...] = act_ref[...]
    for layer in range(2):
        normed[...] = normalize(out_ref[...]).astype(bf16)
        for start in range(0, width, 256):
            cols = pl.ds(start, min(256, width - start))
            update = jnp.dot(normed[...], weights[layer, :, cols], preferred_element_type=f32)
            out_ref[:, cols] = (out_ref[:, cols].astype(f32) + jax.nn.gelu(update)).astype(bf16)


def two_layers(act, weights):
    tokens, width = act.shape
    return pl.pallas_call(
        layers_kernel,
        out_shape=jax.ShapeDtypeStruct(act.shape, bf16),
        in_specs=[VMEM, VMEM],
        out_specs=VMEM,
        scratch_shapes=[pltpu.VMEM(act.shape, bf16)],
        compiler_params=params(24),
        cost_estimate=pl.CostEstimate(
            flops=4 * tokens * width * width, bytes_accessed=4 * width * width, transcendentals=0
        ),
    )(act, weights)


def rows_kernel(scale_ref, act_one, act_two, proj, units, rows_ref):
    width = act_one.shape[1]
    pooled = [jnp.mean(normalize(act[...]), axis=0, keepdims=True) for act in (act_one, act_two)]
    row = lax.broadcasted_iota(jnp.int32, (8, width), 0)
    pooled = jnp.where(row == 0, pooled[0], pooled[1]).astype(bf16)
    emb = lax.dot_general(pooled, proj[...], NT, preferred_element_type=f32)
    rows_ref[...] = scale_ref[0] * lax.dot_general(
        unit_rows(emb), units[...], NT, preferred_element_type=f32
    )


def logit_rows(scale, act_one, act_two, proj, units):
    return pl.pallas_call(
        rows_kernel,
        out_shape=jax.ShapeDtypeStruct((8, units.shape[0]), f32),
        in_specs=[SMEM, VMEM, VMEM, VMEM, VMEM],
        out_specs=VMEM,
        compiler_params=params(24),
    )(scale, act_one, act_two, proj, units)[:2]


def on_device(images, text_pooled, image_weight, proj_image, proj_text, logit_scale, pairing):
    y, zh, zl, x, c = (lax.axis_index(name) for name in AXES)
    width, text_width = proj_image.shape[0], proj_text.shape[0]
    micro = images.shape[0]
    count = pairing.shape[0]

    half = proj_image.shape[1] // 2
    widen = ((0, 0), (0, width - text_width))
    projection = jnp.where(
        y == 3,
        lax.dynamic_slice_in_dim(proj_image, zh * half, half, 1).T,
        jnp.pad(lax.dynamic_slice_in_dim(proj_text, zh * half, half, 1).T, widen),
    )
    texts = jnp.pad(lax.dynamic_slice_in_dim(text_pooled, zh * 2, 2, 0), widen)
    block = jnp.concatenate([image_weight[0], projection, texts])
    rows = image_weight.shape[1]
    spread = lax.all_to_all(
        jnp.broadcast_to(block[None], (8,) + block.shape), ("x", "c"), 0, 0, tiled=True
    )
    weight_rows = spread[:, :rows].reshape(8 * rows, width)
    projection_rows = spread[:, rows:rows + half].reshape(8 * half, width)
    text_rows = spread[:, rows + half:].reshape(TEXTS, width)
    ring = lax.all_gather(
        jnp.where(
            c == 0,
            jnp.concatenate([weight_rows[:FIRST], projection_rows[:FIRST_EXTRA], text_rows]),
            jnp.concatenate([
                weight_rows[FIRST:], projection_rows[FIRST_EXTRA:], jnp.zeros((TEXTS, width), bf16)
            ]),
        ),
        Z + ("c",), axis=0, tiled=True,
    ).reshape(16, 2, BLOCK, width)
    weights = layer_weights(ring)
    units, projection = projection_and_texts(ring, count, text_width)
    units = lax.ppermute(units, "y", [(2, 3)])

    acts = [lax.dynamic_index_in_dim(images, zh * 2 + i, 0, False) for i in range(2)]
    for plane in range(4):
        acts = [two_layers(act, weights) for act in acts]
        if plane < 3:
            acts = [lax.ppermute(act, "y", [(plane, plane + 1)]) for act in acts]
        if plane == 1:
            acts[0], units = lax.optimization_barrier((acts[0], units))
    own_rows = logit_rows(logit_scale, acts[0], acts[1], projection, units)

    other_rows = lax.ppermute(own_rows, "c", [(0, 1), (1, 0)])
    both = jnp.where(
        c == 0, jnp.concatenate([own_rows, other_rows]), jnp.concatenate([other_rows, own_rows])
    )
    of_z = lax.all_to_all(jnp.broadcast_to(both[None], (16, 4, count)), Z, 0, 0, tiled=True)
    logits = lax.all_to_all(
        jnp.broadcast_to(of_z.reshape(1, 64, count), (16, 64, count)), ("y", "x"), 0, 0, tiled=True
    )[12:]
    by_place = logits.reshape(4, 2, 8, 2, 2, count)
    zero = jnp.int32(0)
    own_logits = lax.dynamic_slice(
        by_place, (x, zero, zl, c, zero, zero), (1, 2, 1, 1, 2, count)
    ).reshape(micro, count)
    row_start = ((zl * 4 + x) * 2 + c) * micro
    column_lse = jnp.log(jnp.sum(jnp.exp(logits.reshape(count, count)), axis=0))
    own_pairs = lax.dynamic_slice_in_dim(pairing, row_start, micro, 0)
    paired = own_pairs[:, None] == lax.broadcasted_iota(jnp.int32, (1, count), 1)
    positive = jnp.sum(jnp.where(paired, own_logits, 0.0), axis=1)
    image_loss = jnp.log(jnp.sum(jnp.exp(own_logits), axis=1)) - positive
    text_loss = jnp.sum(jnp.where(paired, column_lse[None, :], 0.0), axis=1) - positive
    columns = count // 8
    logit_block = lax.dynamic_slice_in_dim(own_logits, (y * 2 + zh) * columns, columns, 1)
    return (logit_block, image_loss, text_loss)


def solution(mesh):
    fine = Mesh(mesh.devices.reshape(SIZES), AXES)
    section, dp = ("y", "zh"), ("zl", "x", "c")
    in_specs = (
        P(dp, None, None),
        P(dp, None),
        P(section, dp, None),
        P(None, dp),
        P(None, dp),
        P(),
        P(),
    )
    out_specs = (P(dp, section), P(dp), P(dp))
    return jax.shard_map(on_device, mesh=fine, in_specs=in_specs, out_specs=out_specs, check_vma=False)
```

```python
import functools

import jax
import jax.numpy as jnp
from jax import lax
from jax.experimental import pallas as pl
from jax.experimental.pallas import tpu as pltpu
from jax.sharding import Mesh, PartitionSpec as P

AXES = ("y", "zh", "zl", "x", "c")
SIZES = (4, 2, 8, 4, 2)
Z = ("zh", "zl")
NT = (((1,), (1,)), ((), ()))
bf16, f32 = jnp.bfloat16, jnp.float32
VMEM, ANYWHERE = pl.BlockSpec(memory_space=pltpu.VMEM), pl.BlockSpec(memory_space=pl.ANY)
SMEM = pl.BlockSpec(memory_space=pltpu.SMEM)

FIRST, SECOND, TEXTS = 32, 48, 16


def params(mebibytes):
    return pltpu.CompilerParams(vmem_limit_bytes=mebibytes * 1024 * 1024)


def normalize(values):
    values = values.astype(f32)
    center = jnp.mean(values, axis=-1, keepdims=True)
    spread = jnp.mean((values - center) ** 2, axis=-1, keepdims=True)
    return (values - center) / jnp.sqrt(spread + 1e-05)


def unit_rows(emb):
    square = jnp.sum(emb * emb, axis=1, keepdims=True)
    return (emb / jnp.sqrt(square + 1e-06)).astype(bf16)


def fetch(source, target, sem):
    copy = pltpu.make_async_copy(source, target, sem)
    copy.start()
    return copy


def fetch_projection(ring, proj, sem):
    copies = []
    for z in range(16):
        row = z * (FIRST + SECOND)
        copies += [
            fetch(ring.at[z, 0, pl.ds(0, FIRST), :], proj.at[pl.ds(row, FIRST), :], sem),
            fetch(ring.at[z, 1, pl.ds(0, SECOND), :], proj.at[pl.ds(row + FIRST, SECOND), :], sem),
        ]
    return copies


def texts_kernel(ring, units_ref, proj, texts, sem):
    copies = fetch_projection(ring, proj, sem)
    for z in range(16):
        copies.append(fetch(
            ring.at[z, 0, pl.ds(FIRST, TEXTS), :], texts.at[pl.ds(z * TEXTS, TEXTS), :], sem
        ))
    for copy in copies:
        copy.wait()
    count, width = units_ref.shape
    emb = lax.dot_general(texts[:, :width], proj[:, :width], NT, preferred_element_type=f32)
    held = lax.broadcasted_iota(jnp.int32, (count, count), 1)
    index = ((held >> 1) & 63) * 4 + (held >> 7) * 2 + (held & 1)
    order = (index == lax.broadcasted_iota(jnp.int32, (count, count), 0)).astype(bf16)
    units_ref[...] = jnp.dot(order, unit_rows(emb), preferred_element_type=f32).astype(bf16)


def text_units(ring, count, text_width):
    width = ring.shape[-1]
    rows = 16 * (FIRST + SECOND)
    return pl.pallas_call(
        texts_kernel,
        out_shape=jax.ShapeDtypeStruct((count, text_width), bf16),
        in_specs=[ANYWHERE],
        out_specs=VMEM,
        scratch_shapes=[
            pltpu.VMEM((rows, width), bf16),
            pltpu.VMEM((16 * TEXTS, width), bf16),
            pltpu.SemaphoreType.DMA,
        ],
        compiler_params=params(24),
        cost_estimate=pl.CostEstimate(
            flops=2 * count * text_width * rows, bytes_accessed=2 * rows * width, transcendentals=0
        ),
    )(ring)


def images_kernel(act_one, act_two, ring, units_ref, proj, sem):
    copies = fetch_projection(ring, proj, sem)
    width = act_one.shape[1]
    pooled = [jnp.mean(normalize(act[...]), axis=0, keepdims=True) for act in (act_one, act_two)]
    row = lax.broadcasted_iota(jnp.int32, (16, width), 0)
    pooled = jnp.where(row == 0, pooled[0], pooled[1]).astype(bf16)
    for copy in copies:
        copy.wait()
    units_ref[...] = unit_rows(lax.dot_general(pooled, proj[...], NT, preferred_element_type=f32))


def image_units(act_one, act_two, ring):
    width = ring.shape[-1]
    rows = 16 * (FIRST + SECOND)
    return pl.pallas_call(
        images_kernel,
        out_shape=jax.ShapeDtypeStruct((16, rows), bf16),
        in_specs=[VMEM, VMEM, ANYWHERE],
        out_specs=VMEM,
        scratch_shapes=[pltpu.VMEM((rows, width), bf16), pltpu.SemaphoreType.DMA],
        compiler_params=params(24),
        cost_estimate=pl.CostEstimate(
            flops=32 * rows * width, bytes_accessed=2 * rows * width, transcendentals=0
        ),
    )(act_one, act_two, ring)


def layers_kernel(act_ref, weights, out_ref, normed):
    width = act_ref.shape[1]
    out_ref[...] = act_ref[...]
    for layer in range(2):
        normed[...] = normalize(out_ref[...]).astype(bf16)
        for start in range(0, width, 256):
            cols = pl.ds(start, min(256, width - start))
            update = jnp.dot(normed[...], weights[layer, :, cols], preferred_element_type=f32)
            out_ref[:, cols] = (out_ref[:, cols].astype(f32) + jax.nn.gelu(update)).astype(bf16)


def two_layers(act, weights):
    tokens, width = act.shape
    return pl.pallas_call(
        layers_kernel,
        out_shape=jax.ShapeDtypeStruct(act.shape, bf16),
        in_specs=[VMEM, VMEM],
        out_specs=VMEM,
        scratch_shapes=[pltpu.VMEM(act.shape, bf16)],
        compiler_params=params(24),
        cost_estimate=pl.CostEstimate(
            flops=4 * tokens * width * width, bytes_accessed=4 * width * width, transcendentals=0
        ),
    )(act, weights)


def on_device(images, text_pooled, image_weight, proj_image, proj_text, logit_scale, pairing):
    y, zh, zl, x, c = (lax.axis_index(name) for name in AXES)
    width, text_width = proj_image.shape[0], proj_text.shape[0]
    micro = images.shape[0]
    count = pairing.shape[0]

    half = proj_image.shape[1] // 2
    widen = ((0, 0), (0, width - text_width))
    projection = jnp.where(
        y == 3,
        lax.dynamic_slice_in_dim(proj_image, zh * half, half, 1).T,
        jnp.pad(lax.dynamic_slice_in_dim(proj_text, zh * half, half, 1).T, widen),
    )
    texts = jnp.pad(lax.dynamic_slice_in_dim(text_pooled, zh * 2, 2, 0), widen)
    extra = jnp.concatenate([projection, texts])

    def spread(block):
        return lax.all_to_all(
            jnp.broadcast_to(block[None], (8,) + block.shape), ("x", "c"), 0, 0, tiled=True
        )

    def of_core(first, second):
        return jnp.where(c == 0, first, second)

    def round_z(block):
        return lax.all_gather(block, Z + ("c",), axis=0, tiled=True)

    rows = spread(image_weight[0]).reshape(-1, width)
    part = rows.shape[0] // 2
    part_rows, extra = lax.optimization_barrier((of_core(rows[:part], rows[part:]), extra))
    weights = round_z(part_rows)
    extra = spread(extra)
    projection, texts = extra[:, :half].reshape(8 * half, width), extra[:, half:].reshape(TEXTS, width)
    extra = of_core(jnp.concatenate([projection[:FIRST], texts]), projection[FIRST:])
    weights, extra = lax.optimization_barrier((weights, extra))
    weights = weights.reshape(2, width, width)
    ring = round_z(extra).reshape(16, 2, SECOND, width)

    acts = [lax.dynamic_index_in_dim(images, zh * 2 + i, 0, False) for i in range(2)]
    for plane in range(4):
        acts = [two_layers(act, weights) for act in acts]
        if plane < 3:
            acts = [lax.ppermute(act, "y", [(plane, plane + 1)]) for act in acts]
    ring, acts = lax.optimization_barrier((ring, acts))
    images_back = lax.ppermute(image_units(acts[0], acts[1], ring), "y", [(3, 2)])
    own_rows = logit_scale[0] * lax.dot_general(
        images_back, text_units(ring, count, text_width), NT, preferred_element_type=f32
    )[:2]

    of_z = lax.all_to_all(jnp.broadcast_to(own_rows[None], (16, 2, count)), Z, 0, 0, tiled=True)
    by_place = of_z.reshape(2, 8, 2, count)
    zero = jnp.int32(0)
    of_dp = lax.dynamic_slice(by_place, (zero, zl, zero, zero), (2, 1, 2, count)).reshape(micro, count)
    sums = jnp.sum(jnp.exp(of_z), axis=(0, 1))
    sent = jnp.concatenate([of_dp, sums[None]])
    from_plane = lax.all_to_all(
        jnp.broadcast_to(sent[None], (16,) + sent.shape), ("y", "x"), 0, 0, tiled=True
    )[8:12]
    own_logits = lax.dynamic_index_in_dim(from_plane, x, 0, False)[:micro]
    column_lse = jnp.log(lax.psum(jnp.sum(from_plane[:, micro], axis=0), "c"))
    row_start = ((zl * 4 + x) * 2 + c) * micro
    own_pairs = lax.dynamic_slice_in_dim(pairing, row_start, micro, 0)
    paired = own_pairs[:, None] == lax.broadcasted_iota(jnp.int32, (1, count), 1)
    positive = jnp.sum(jnp.where(paired, own_logits, 0.0), axis=1)
    image_loss = jnp.log(jnp.sum(jnp.exp(own_logits), axis=1)) - positive
    text_loss = jnp.sum(jnp.where(paired, column_lse[None, :], 0.0), axis=1) - positive
    columns = count // 8
    logit_block = lax.dynamic_slice_in_dim(own_logits, (y * 2 + zh) * columns, columns, 1)
    return (logit_block, image_loss, text_loss)


def solution(mesh):
    fine = Mesh(mesh.devices.reshape(SIZES), AXES)
    section, dp = ("y", "zh"), ("zl", "x", "c")
    in_specs = (
        P(dp, None, None),
        P(dp, None),
        P(section, dp, None),
        P(None, dp),
        P(None, dp),
        P(),
        P(),
    )
    out_specs = (P(dp, section), P(dp), P(dp))
    return jax.shard_map(on_device, mesh=fine, in_specs=in_specs, out_specs=out_specs, check_vma=False)
```

```python
import functools

import jax
import jax.numpy as jnp
from jax import lax
from jax.experimental import pallas as pl
from jax.experimental.pallas import tpu as pltpu
from jax.sharding import Mesh, PartitionSpec as P

AXES = ("y", "zh", "zl", "x", "c")
SIZES = (4, 2, 8, 4, 2)
Z = ("zh", "zl")
NT = (((1,), (1,)), ((), ()))
bf16, f32 = jnp.bfloat16, jnp.float32
VMEM, ANYWHERE = pl.BlockSpec(memory_space=pltpu.VMEM), pl.BlockSpec(memory_space=pl.ANY)
SMEM = pl.BlockSpec(memory_space=pltpu.SMEM)

PROJECTION, TEXTS = 160, 32


def params(mebibytes):
    return pltpu.CompilerParams(vmem_limit_bytes=mebibytes * 1024 * 1024)


def normalize(values):
    values = values.astype(f32)
    center = jnp.mean(values, axis=-1, keepdims=True)
    spread = jnp.mean((values - center) ** 2, axis=-1, keepdims=True)
    return (values - center) / jnp.sqrt(spread + 1e-05)


def unit_rows(emb):
    square = jnp.sum(emb * emb, axis=1, keepdims=True)
    return (emb / jnp.sqrt(square + 1e-06)).astype(bf16)


def fetch(source, target, sem):
    copy = pltpu.make_async_copy(source, target, sem)
    copy.start()
    return copy


def fetch_rows(held, start, target, sem):
    count = target.shape[0] // 8
    return [
        fetch(held.at[i, pl.ds(start, count), :], target.at[pl.ds(i * count, count), :], sem)
        for i in range(8)
    ]


def texts_kernel(held, units_ref, proj, texts, sem):
    for copy in fetch_rows(held, 0, proj, sem) + fetch_rows(held, PROJECTION, texts, sem):
        copy.wait()
    count, width = units_ref.shape
    emb = lax.dot_general(texts[:, :width], proj[:, :width], NT, preferred_element_type=f32)
    place = lax.broadcasted_iota(jnp.int32, (count, count), 1)
    index = ((place >> 1) & 7) * 32 + (place >> 5) * 4 + ((place >> 4) & 1) * 2 + (place & 1)
    order = (index == lax.broadcasted_iota(jnp.int32, (count, count), 0)).astype(bf16)
    units_ref[...] = jnp.dot(order, unit_rows(emb), preferred_element_type=f32).astype(bf16)


def text_units(held, count, text_width):
    width = held.shape[-1]
    rows = 8 * PROJECTION
    return pl.pallas_call(
        texts_kernel,
        out_shape=jax.ShapeDtypeStruct((count, text_width), bf16),
        in_specs=[ANYWHERE],
        out_specs=VMEM,
        scratch_shapes=[
            pltpu.VMEM((rows, width), bf16),
            pltpu.VMEM((8 * TEXTS, width), bf16),
            pltpu.SemaphoreType.DMA,
        ],
        compiler_params=params(52),
        cost_estimate=pl.CostEstimate(
            flops=2 * count * text_width * rows, bytes_accessed=2 * rows * width, transcendentals=0
        ),
    )(held)


def images_kernel(*refs):
    acts, (held, units_ref, proj, sem) = refs[:-4], refs[-4:]
    copies = fetch_rows(held, 0, proj, sem)
    width = acts[0].shape[1]
    tokens = 2 * acts[0].shape[0]
    sums = [jnp.sum(normalize(act[...]), axis=0, keepdims=True) for act in acts]
    row = lax.broadcasted_iota(jnp.int32, (16, width), 0)
    pooled = jnp.where(row == 0, sums[0] + sums[1], sums[2] + sums[3])
    pooled = (pooled / tokens).astype(bf16)
    for copy in copies:
        copy.wait()
    units_ref[...] = unit_rows(lax.dot_general(pooled, proj[...], NT, preferred_element_type=f32))


def image_units(acts, held):
    width = held.shape[-1]
    rows = 8 * PROJECTION
    return pl.pallas_call(
        images_kernel,
        out_shape=jax.ShapeDtypeStruct((16, rows), bf16),
        in_specs=[VMEM] * 4 + [ANYWHERE],
        out_specs=VMEM,
        scratch_shapes=[pltpu.VMEM((rows, width), bf16), pltpu.SemaphoreType.DMA],
        compiler_params=params(52),
        cost_estimate=pl.CostEstimate(
            flops=32 * rows * width, bytes_accessed=2 * rows * width, transcendentals=0
        ),
    )(*acts, held)


def layers_kernel(act_ref, weights, out_ref, normed):
    width = act_ref.shape[1]
    out_ref[...] = act_ref[...]
    for layer in range(2):
        normed[...] = normalize(out_ref[...]).astype(bf16)
        for start in range(0, width, 256):
            cols = pl.ds(start, min(256, width - start))
            update = jnp.dot(normed[...], weights[layer, :, cols], preferred_element_type=f32)
            out_ref[:, cols] = (out_ref[:, cols].astype(f32) + jax.nn.gelu(update)).astype(bf16)


def two_layers(act, weights):
    tokens, width = act.shape
    return pl.pallas_call(
        layers_kernel,
        out_shape=jax.ShapeDtypeStruct(act.shape, bf16),
        in_specs=[VMEM, VMEM],
        out_specs=VMEM,
        scratch_shapes=[pltpu.VMEM(act.shape, bf16)],
        compiler_params=params(24),
        cost_estimate=pl.CostEstimate(
            flops=4 * tokens * width * width, bytes_accessed=4 * width * width, transcendentals=0
        ),
    )(act, weights)


def on_device(images, text_pooled, image_weight, proj_image, proj_text, logit_scale, pairing):
    y, zh, zl, x, c = (lax.axis_index(name) for name in AXES)
    width, text_width = proj_image.shape[0], proj_text.shape[0]
    micro = images.shape[0]
    count = pairing.shape[0]

    half = proj_image.shape[1] // 2
    widen = ((0, 0), (0, width - text_width))
    projection = jnp.where(
        y == 3,
        lax.dynamic_slice_in_dim(proj_image, zh * half, half, 1).T,
        jnp.pad(lax.dynamic_slice_in_dim(proj_text, zh * half, half, 1).T, widen),
    )
    texts = jnp.pad(lax.dynamic_slice_in_dim(text_pooled, zh * 2, 2, 0), widen)
    rows = lax.all_to_all(
        jnp.broadcast_to(image_weight, (8,) + image_weight.shape[1:]), ("x", "c"), 0, 0, tiled=True
    ).reshape(-1, width)
    half_rows = rows.shape[0] // 2
    rows = jnp.where(c == 0, rows[:half_rows], rows[half_rows:])
    rows, projection, texts = lax.optimization_barrier((rows, projection, texts))
    weights = lax.all_gather(rows, Z + ("c",), axis=0, tiled=True)

    ring = lax.all_gather(jnp.concatenate([projection, texts]), Z, axis=0)
    ring = jnp.concatenate([
        ring[:, :half].reshape(PROJECTION, width), ring[:, half:].reshape(TEXTS, width)
    ])
    weights, ring = lax.optimization_barrier((weights, ring))
    weights = weights.reshape(2, width, width)
    held = lax.all_gather(ring, ("x", "c"), axis=0)

    part = images.shape[1] // 2
    acts = [
        lax.dynamic_slice(images, (zh * 2 + i, j * part, 0), (1, part, width))[0]
        for i in range(2) for j in range(2)
    ]
    for plane in range(4):
        for i in range(4):
            acts[i] = two_layers(acts[i], weights)
            if plane < 3:
                acts[i] = lax.ppermute(acts[i], "y", [(plane, plane + 1)])
    held, acts = lax.optimization_barrier((held, acts))
    images_back = lax.ppermute(image_units(acts, held), "y", [(3, 2)])
    own_rows = logit_scale[0] * lax.dot_general(
        images_back, text_units(held, count, text_width), NT, preferred_element_type=f32
    )[:2]

    of_z = lax.all_to_all(jnp.broadcast_to(own_rows[None], (16, 2, count)), Z, 0, 0, tiled=True)
    by_place = of_z.reshape(2, 8, 2, count)
    zero = jnp.int32(0)
    of_dp = lax.dynamic_slice(by_place, (zero, zl, zero, zero), (2, 1, 2, count)).reshape(micro, count)
    sums = jnp.sum(jnp.exp(of_z), axis=(0, 1))
    sent = jnp.concatenate([of_dp, sums[None]])
    from_plane = lax.all_to_all(
        jnp.broadcast_to(sent[None], (16,) + sent.shape), ("y", "x"), 0, 0, tiled=True
    )[8:12]
    own_logits = lax.dynamic_index_in_dim(from_plane, x, 0, False)[:micro]
    column_lse = jnp.log(lax.psum(jnp.sum(from_plane[:, micro], axis=0), "c"))
    row_start = ((zl * 4 + x) * 2 + c) * micro
    own_pairs = lax.dynamic_slice_in_dim(pairing, row_start, micro, 0)
    paired = own_pairs[:, None] == lax.broadcasted_iota(jnp.int32, (1, count), 1)
    positive = jnp.sum(jnp.where(paired, own_logits, 0.0), axis=1)
    image_loss = jnp.log(jnp.sum(jnp.exp(own_logits), axis=1)) - positive
    text_loss = jnp.sum(jnp.where(paired, column_lse[None, :], 0.0), axis=1) - positive
    columns = count // 8
    logit_block = lax.dynamic_slice_in_dim(own_logits, (y * 2 + zh) * columns, columns, 1)
    return (logit_block, image_loss, text_loss)


def solution(mesh):
    fine = Mesh(mesh.devices.reshape(SIZES), AXES)
    section, dp = ("y", "zh"), ("zl", "x", "c")
    in_specs = (
        P(dp, None, None),
        P(dp, None),
        P(section, dp, None),
        P(None, dp),
        P(None, dp),
        P(),
        P(),
    )
    out_specs = (P(dp, section), P(dp), P(dp))
    return jax.shard_map(on_device, mesh=fine, in_specs=in_specs, out_specs=out_specs, check_vma=False)
```

```python
import functools

import jax
import jax.numpy as jnp
from jax import lax
from jax.experimental import pallas as pl
from jax.experimental.pallas import tpu as pltpu
from jax.sharding import Mesh, PartitionSpec as P

AXES = ("y", "zh", "zl", "x", "c")
SIZES = (4, 2, 8, 4, 2)
Z = ("zh", "zl")
NT = (((1,), (1,)), ((), ()))
bf16, f32 = jnp.bfloat16, jnp.float32
VMEM, ANYWHERE = pl.BlockSpec(memory_space=pltpu.VMEM), pl.BlockSpec(memory_space=pl.ANY)
SMEM = pl.BlockSpec(memory_space=pltpu.SMEM)

PROJECTION, TEXTS = 160, 32


def params(mebibytes):
    return pltpu.CompilerParams(vmem_limit_bytes=mebibytes * 1024 * 1024)


def normalize(values):
    values = values.astype(f32)
    center = jnp.mean(values, axis=-1, keepdims=True)
    spread = jnp.mean((values - center) ** 2, axis=-1, keepdims=True)
    return (values - center) / jnp.sqrt(spread + 1e-05)


def unit_rows(emb):
    square = jnp.sum(emb * emb, axis=1, keepdims=True)
    return (emb / jnp.sqrt(square + 1e-06)).astype(bf16)


def fetch(source, target, sem):
    copy = pltpu.make_async_copy(source, target, sem)
    copy.start()
    return copy


def fetch_rows(held, start, target, sem):
    count = target.shape[0] // 8
    return [
        fetch(held.at[i, pl.ds(start, count), :], target.at[pl.ds(i * count, count), :], sem)
        for i in range(8)
    ]


def texts_kernel(held, units_ref, proj, texts, sem):
    for copy in fetch_rows(held, 0, proj, sem) + fetch_rows(held, PROJECTION, texts, sem):
        copy.wait()
    count, width = units_ref.shape
    emb = lax.dot_general(texts[:, :width], proj[:, :width], NT, preferred_element_type=f32)
    place = lax.broadcasted_iota(jnp.int32, (count, count), 1)
    index = ((place >> 1) & 7) * 32 + (place >> 5) * 4 + ((place >> 4) & 1) * 2 + (place & 1)
    order = (index == lax.broadcasted_iota(jnp.int32, (count, count), 0)).astype(bf16)
    units_ref[...] = jnp.dot(order, unit_rows(emb), preferred_element_type=f32).astype(bf16)


def text_units(held, count, text_width):
    width = held.shape[-1]
    rows = 8 * PROJECTION
    return pl.pallas_call(
        texts_kernel,
        out_shape=jax.ShapeDtypeStruct((count, text_width), bf16),
        in_specs=[ANYWHERE],
        out_specs=VMEM,
        scratch_shapes=[
            pltpu.VMEM((rows, width), bf16),
            pltpu.VMEM((8 * TEXTS, width), bf16),
            pltpu.SemaphoreType.DMA,
        ],
        compiler_params=params(52),
        cost_estimate=pl.CostEstimate(
            flops=2 * count * text_width * rows, bytes_accessed=2 * rows * width, transcendentals=0
        ),
    )(held)


def images_kernel(*refs):
    acts, (held, units_ref, proj, sem) = refs[:-4], refs[-4:]
    copies = fetch_rows(held, 0, proj, sem)
    width = acts[0].shape[1]
    tokens = 2 * acts[0].shape[0]
    sums = [jnp.sum(normalize(act[...]), axis=0, keepdims=True) for act in acts]
    row = lax.broadcasted_iota(jnp.int32, (16, width), 0)
    pooled = jnp.where(row == 0, sums[0] + sums[1], sums[2] + sums[3])
    pooled = (pooled / tokens).astype(bf16)
    for copy in copies:
        copy.wait()
    units_ref[...] = unit_rows(lax.dot_general(pooled, proj[...], NT, preferred_element_type=f32))


def image_units(acts, held):
    width = held.shape[-1]
    rows = 8 * PROJECTION
    return pl.pallas_call(
        images_kernel,
        out_shape=jax.ShapeDtypeStruct((16, rows), bf16),
        in_specs=[VMEM] * 4 + [ANYWHERE],
        out_specs=VMEM,
        scratch_shapes=[pltpu.VMEM((rows, width), bf16), pltpu.SemaphoreType.DMA],
        compiler_params=params(52),
        cost_estimate=pl.CostEstimate(
            flops=32 * rows * width, bytes_accessed=2 * rows * width, transcendentals=0
        ),
    )(*acts, held)


def layer_step(layer, act, weights, normed):
    width = act.shape[1]
    normed[...] = normalize(act[...]).astype(bf16)
    for start in range(0, width, 256):
        cols = pl.ds(start, min(256, width - start))
        update = jnp.dot(normed[...], weights[layer, :, cols], preferred_element_type=f32)
        act[:, cols] = (act[:, cols].astype(f32) + jax.nn.gelu(update)).astype(bf16)


def layers_kernel(plane, y_ref, act_ref, weights, out_ref, normed):
    out_ref[...] = act_ref[...]

    @pl.when(y_ref[0] == plane)
    def _():
        for layer in range(2):
            layer_step(layer, out_ref, weights, normed)


def two_layers(plane, y, act, weights):
    tokens, width = act.shape
    return pl.pallas_call(
        functools.partial(layers_kernel, plane),
        out_shape=jax.ShapeDtypeStruct(act.shape, bf16),
        in_specs=[SMEM, VMEM, VMEM],
        out_specs=VMEM,
        scratch_shapes=[pltpu.VMEM(act.shape, bf16)],
        compiler_params=params(24),
        cost_estimate=pl.CostEstimate(
            flops=4 * tokens * width * width, bytes_accessed=4 * width * width, transcendentals=0
        ),
    )(y, act, weights)


def on_device(images, text_pooled, image_weight, proj_image, proj_text, logit_scale, pairing):
    y, zh, zl, x, c = (lax.axis_index(name) for name in AXES)
    width, text_width = proj_image.shape[0], proj_text.shape[0]
    micro = images.shape[0]
    count = pairing.shape[0]

    half = proj_image.shape[1] // 2
    widen = ((0, 0), (0, width - text_width))
    projection = jnp.where(
        y == 3,
        lax.dynamic_slice_in_dim(proj_image, zh * half, half, 1).T,
        jnp.pad(lax.dynamic_slice_in_dim(proj_text, zh * half, half, 1).T, widen),
    )
    texts = jnp.pad(lax.dynamic_slice_in_dim(text_pooled, zh * 2, 2, 0), widen)
    rows = lax.all_gather(image_weight[0], ("x", "c"), axis=0).reshape(-1, width)
    half_rows = rows.shape[0] // 2
    rows = jnp.where(c == 0, rows[:half_rows], rows[half_rows:])
    rows, projection, texts = lax.optimization_barrier((rows, projection, texts))
    weights = lax.all_gather(rows, Z + ("c",), axis=0, tiled=True)

    ring = lax.all_gather(jnp.concatenate([projection, texts]), Z, axis=0)
    ring = jnp.concatenate([
        ring[:, :half].reshape(PROJECTION, width), ring[:, half:].reshape(TEXTS, width)
    ])
    weights, ring = lax.optimization_barrier((weights, ring))
    weights = weights.reshape(2, width, width)
    held = lax.all_gather(ring, ("x", "c"), axis=0)

    part = images.shape[1] // 2
    acts = [
        lax.dynamic_slice(images, (zh * 2 + i, j * part, 0), (1, part, width))[0]
        for i in range(2) for j in range(2)
    ]
    for plane in range(4):
        for i in range(4):
            acts[i] = two_layers(plane, y.astype(jnp.int32)[None], acts[i], weights)
            if plane < 3:
                acts[i] = lax.ppermute(acts[i], "y", [(plane, plane + 1)])
    held, acts = lax.optimization_barrier((held, acts))
    images_back = lax.ppermute(image_units(acts, held), "y", [(3, 2)])
    own_rows = logit_scale[0] * lax.dot_general(
        images_back, text_units(held, count, text_width), NT, preferred_element_type=f32
    )[:2]

    of_z = lax.all_to_all(jnp.broadcast_to(own_rows[None], (16, 2, count)), Z, 0, 0, tiled=True)
    by_place = of_z.reshape(2, 8, 2, count)
    zero = jnp.int32(0)
    of_dp = lax.dynamic_slice(by_place, (zero, zl, zero, zero), (2, 1, 2, count)).reshape(micro, count)
    sums = jnp.sum(jnp.exp(of_z), axis=(0, 1))
    sent = jnp.concatenate([of_dp, sums[None]])
    from_plane = lax.all_to_all(
        jnp.broadcast_to(sent[None], (16,) + sent.shape), ("y", "x"), 0, 0, tiled=True
    )[8:12]
    own_logits = lax.dynamic_index_in_dim(from_plane, x, 0, False)[:micro]
    column_lse = jnp.log(lax.psum(jnp.sum(from_plane[:, micro], axis=0), "c"))
    row_start = ((zl * 4 + x) * 2 + c) * micro
    own_pairs = lax.dynamic_slice_in_dim(pairing, row_start, micro, 0)
    paired = own_pairs[:, None] == lax.broadcasted_iota(jnp.int32, (1, count), 1)
    positive = jnp.sum(jnp.where(paired, own_logits, 0.0), axis=1)
    image_loss = jnp.log(jnp.sum(jnp.exp(own_logits), axis=1)) - positive
    text_loss = jnp.sum(jnp.where(paired, column_lse[None, :], 0.0), axis=1) - positive
    columns = count // 8
    logit_block = lax.dynamic_slice_in_dim(own_logits, (y * 2 + zh) * columns, columns, 1)
    return (logit_block, image_loss, text_loss)


def solution(mesh):
    fine = Mesh(mesh.devices.reshape(SIZES), AXES)
    section, dp = ("y", "zh"), ("zl", "x", "c")
    in_specs = (
        P(dp, None, None),
        P(dp, None),
        P(section, dp, None),
        P(None, dp),
        P(None, dp),
        P(),
        P(),
    )
    out_specs = (P(dp, section), P(dp), P(dp))
    return jax.shard_map(on_device, mesh=fine, in_specs=in_specs, out_specs=out_specs, check_vma=False)
```

```python
import functools

import jax
import jax.numpy as jnp
from jax import lax
from jax.experimental import pallas as pl
from jax.experimental.pallas import tpu as pltpu
from jax.sharding import Mesh, PartitionSpec as P

AXES = ("y", "zh", "zl", "x", "c")
SIZES = (4, 2, 8, 4, 2)
Z = ("zh", "zl")
NT = (((1,), (1,)), ((), ()))
bf16, f32 = jnp.bfloat16, jnp.float32
VMEM, ANYWHERE = pl.BlockSpec(memory_space=pltpu.VMEM), pl.BlockSpec(memory_space=pl.ANY)
SMEM = pl.BlockSpec(memory_space=pltpu.SMEM)

PROJECTION, TEXTS = 160, 32
SIDE = 32


def params(mebibytes):
    return pltpu.CompilerParams(vmem_limit_bytes=mebibytes * 1024 * 1024)


def normalize(values):
    values = values.astype(f32)
    center = jnp.mean(values, axis=-1, keepdims=True)
    spread = jnp.mean((values - center) ** 2, axis=-1, keepdims=True)
    return (values - center) / jnp.sqrt(spread + 1e-05)


def unit_rows(emb):
    square = jnp.sum(emb * emb, axis=1, keepdims=True)
    return (emb / jnp.sqrt(square + 1e-06)).astype(bf16)


def fetch(source, target, sem):
    copy = pltpu.make_async_copy(source, target, sem)
    copy.start()
    return copy


def fetch_rows(held, start, target, sem):
    count = target.shape[0] // 8
    return [
        fetch(held.at[i, pl.ds(start, count), :], target.at[pl.ds(i * count, count), :], sem)
        for i in range(8)
    ]


def texts_kernel(held, units_ref, proj, texts, sem):
    for copy in fetch_rows(held, 0, proj, sem) + fetch_rows(held, PROJECTION, texts, sem):
        copy.wait()
    count, width = units_ref.shape
    emb = lax.dot_general(texts[:, :width], proj[:, :width], NT, preferred_element_type=f32)
    place = lax.broadcasted_iota(jnp.int32, (count, count), 1)
    index = ((place >> 1) & 7) * 32 + (place >> 5) * 4 + ((place >> 4) & 1) * 2 + (place & 1)
    order = (index == lax.broadcasted_iota(jnp.int32, (count, count), 0)).astype(bf16)
    units_ref[...] = jnp.dot(order, unit_rows(emb), preferred_element_type=f32).astype(bf16)


def text_units(held, count, text_width):
    width = held.shape[-1]
    rows = 8 * PROJECTION
    return pl.pallas_call(
        texts_kernel,
        out_shape=jax.ShapeDtypeStruct((count, text_width), bf16),
        in_specs=[ANYWHERE],
        out_specs=VMEM,
        scratch_shapes=[
            pltpu.VMEM((rows, width), bf16),
            pltpu.VMEM((8 * TEXTS, width), bf16),
            pltpu.SemaphoreType.DMA,
        ],
        compiler_params=params(52),
        cost_estimate=pl.CostEstimate(
            flops=2 * count * text_width * rows, bytes_accessed=2 * rows * width, transcendentals=0
        ),
    )(held)


def images_kernel(tokens, *refs):
    sums, (held, units_ref, proj, sem) = refs[:-4], refs[-4:]
    copies = fetch_rows(held, 0, proj, sem)
    row = lax.broadcasted_iota(jnp.int32, (16, held.shape[-1]), 0)
    pooled = jnp.where(row == 0, sums[0][:1] + sums[1][:1], sums[2][:1] + sums[3][:1])
    pooled = (pooled / tokens).astype(bf16)
    for copy in copies:
        copy.wait()
    units_ref[...] = unit_rows(lax.dot_general(pooled, proj[...], NT, preferred_element_type=f32))


def image_units(sums, held, tokens):
    width = held.shape[-1]
    rows = 8 * PROJECTION
    return pl.pallas_call(
        functools.partial(images_kernel, tokens),
        out_shape=jax.ShapeDtypeStruct((16, rows), bf16),
        in_specs=[VMEM] * 4 + [ANYWHERE],
        out_specs=VMEM,
        scratch_shapes=[pltpu.VMEM((rows, width), bf16), pltpu.SemaphoreType.DMA],
        compiler_params=params(52),
        cost_estimate=pl.CostEstimate(
            flops=32 * rows * width, bytes_accessed=2 * rows * width, transcendentals=0
        ),
    )(*sums, held)


def layers_kernel(plane, last, y_ref, act_ref, ring, side, out_ref, act, normed_ring, normed_side):
    width = act_ref.shape[1]
    ring_rows, side_rows = ring.shape[1] // 8, side.shape[1] // 8
    act[...] = act_ref[...]

    @pl.when(y_ref[0] == plane)
    def _():
        for layer in range(2):
            normed = normalize(act[...]).astype(bf16)
            for zl in range(8):
                start = zl * (ring_rows + side_rows)
                middle, end = start + ring_rows, start + ring_rows + side_rows
                normed_ring[:, zl * ring_rows:(zl + 1) * ring_rows] = normed[:, start:middle]
                normed_side[:, zl * side_rows:(zl + 1) * side_rows] = normed[:, middle:end]
            for start in range(0, width, 256):
                cols = pl.ds(start, min(256, width - start))
                update = jnp.dot(normed_ring[...], ring[layer, :, cols], preferred_element_type=f32)
                update += jnp.dot(normed_side[...], side[layer, :, cols], preferred_element_type=f32)
                act[:, cols] = (act[:, cols].astype(f32) + jax.nn.gelu(update)).astype(bf16)

    if last:
        total = jnp.sum(normalize(act[...]), axis=0, keepdims=True)
        out_ref[...] = jnp.broadcast_to(total, out_ref.shape)
    else:
        out_ref[...] = act[...]


def two_layers(plane, last, y, act, weights):
    tokens, width = act.shape
    out_shape = jax.ShapeDtypeStruct((8, width), f32) if last else jax.ShapeDtypeStruct(act.shape, bf16)
    return pl.pallas_call(
        functools.partial(layers_kernel, plane, last),
        out_shape=out_shape,
        in_specs=[SMEM, VMEM, VMEM, VMEM],
        out_specs=VMEM,
        scratch_shapes=[pltpu.VMEM(act.shape, bf16)] + [
            pltpu.VMEM((tokens, part.shape[1]), bf16) for part in weights
        ],
        compiler_params=params(24),
        cost_estimate=pl.CostEstimate(
            flops=4 * tokens * width * width, bytes_accessed=4 * width * width, transcendentals=0
        ),
    )(y, act, *weights)


def on_device(images, text_pooled, image_weight, proj_image, proj_text, logit_scale, pairing):
    y, zh, zl, x, c = (lax.axis_index(name) for name in AXES)
    width, text_width = proj_image.shape[0], proj_text.shape[0]
    micro = images.shape[0]
    count = pairing.shape[0]

    half = proj_image.shape[1] // 2
    widen = ((0, 0), (0, width - text_width))
    projection = jnp.where(
        y == 3,
        lax.dynamic_slice_in_dim(proj_image, zh * half, half, 1).T,
        jnp.pad(lax.dynamic_slice_in_dim(proj_text, zh * half, half, 1).T, widen),
    )
    texts = jnp.pad(lax.dynamic_slice_in_dim(text_pooled, zh * 2, 2, 0), widen)
    rows = lax.all_gather(image_weight[0], ("x", "c"), axis=0).reshape(-1, width)
    def of_core(values):
        middle = values.shape[0] // 2
        return jnp.where(c == 0, values[:middle], values[middle:])

    ring, side = of_core(rows[:-SIDE]), of_core(rows[-SIDE:])
    ring, side, projection, texts = lax.optimization_barrier((ring, side, projection, texts))
    ring = lax.all_gather(ring, Z + ("c",), axis=0, tiled=True)
    side = lax.all_gather(side, Z, axis=0)
    other = lax.ppermute(side, "c", [(0, 1), (1, 0)])
    other, projection, texts = lax.optimization_barrier((other, projection, texts))
    side = jnp.stack([jnp.where(c == 0, side, other), jnp.where(c == 0, other, side)], axis=1)
    side = side.reshape(2, 8 * SIDE, width)

    extra = lax.all_gather(jnp.concatenate([projection, texts]), Z, axis=0)
    extra = jnp.concatenate([
        extra[:, :half].reshape(PROJECTION, width), extra[:, half:].reshape(TEXTS, width)
    ])
    ring, extra = lax.optimization_barrier((ring, extra))
    weights = (ring.reshape(2, -1, width), side)
    held = lax.all_gather(extra, ("x", "c"), axis=0)

    part = images.shape[1] // 2
    acts = [
        lax.dynamic_slice(images, (zh * 2 + i, j * part, 0), (1, part, width))[0]
        for i in range(2) for j in range(2)
    ]
    for plane in range(4):
        for i in range(4):
            acts[i] = two_layers(plane, plane == 3, y.astype(jnp.int32)[None], acts[i], weights)
            if plane < 3:
                acts[i] = lax.ppermute(acts[i], "y", [(plane, plane + 1)])
    held, acts = lax.optimization_barrier((held, acts))
    images_back = lax.ppermute(image_units(acts, held, images.shape[1]), "y", [(3, 2)])
    own_rows = logit_scale[0] * lax.dot_general(
        images_back, text_units(held, count, text_width), NT, preferred_element_type=f32
    )[:2]

    of_z = lax.all_to_all(jnp.broadcast_to(own_rows[None], (16, 2, count)), Z, 0, 0, tiled=True)
    by_place = of_z.reshape(2, 8, 2, count)
    zero = jnp.int32(0)
    of_dp = lax.dynamic_slice(by_place, (zero, zl, zero, zero), (2, 1, 2, count)).reshape(micro, count)
    sums = jnp.sum(jnp.exp(of_z), axis=(0, 1))
    sent = jnp.concatenate([of_dp, sums[None]])
    from_plane = lax.all_to_all(
        jnp.broadcast_to(sent[None], (16,) + sent.shape), ("y", "x"), 0, 0, tiled=True
    )[8:12]
    own_logits = lax.dynamic_index_in_dim(from_plane, x, 0, False)[:micro]
    column_lse = jnp.log(lax.psum(jnp.sum(from_plane[:, micro], axis=0), "c"))
    row_start = ((zl * 4 + x) * 2 + c) * micro
    own_pairs = lax.dynamic_slice_in_dim(pairing, row_start, micro, 0)
    paired = own_pairs[:, None] == lax.broadcasted_iota(jnp.int32, (1, count), 1)
    positive = jnp.sum(jnp.where(paired, own_logits, 0.0), axis=1)
    image_loss = jnp.log(jnp.sum(jnp.exp(own_logits), axis=1)) - positive
    text_loss = jnp.sum(jnp.where(paired, column_lse[None, :], 0.0), axis=1) - positive
    columns = count // 8
    logit_block = lax.dynamic_slice_in_dim(own_logits, (y * 2 + zh) * columns, columns, 1)
    return (logit_block, image_loss, text_loss)


def solution(mesh):
    fine = Mesh(mesh.devices.reshape(SIZES), AXES)
    section, dp = ("y", "zh"), ("zl", "x", "c")
    in_specs = (
        P(dp, None, None),
        P(dp, None),
        P(section, dp, None),
        P(None, dp),
        P(None, dp),
        P(),
        P(),
    )
    out_specs = (P(dp, section), P(dp), P(dp))
    return jax.shard_map(on_device, mesh=fine, in_specs=in_specs, out_specs=out_specs, check_vma=False)
```

```python
import functools

import jax
import jax.numpy as jnp
from jax import lax
from jax.experimental import pallas as pl
from jax.experimental.pallas import tpu as pltpu
from jax.sharding import Mesh, PartitionSpec as P

AXES = ("y", "zh", "zl", "x", "c")
SIZES = (4, 2, 8, 4, 2)
Z = ("zh", "zl")
NT = (((1,), (1,)), ((), ()))
bf16, f32 = jnp.bfloat16, jnp.float32
VMEM, ANYWHERE = pl.BlockSpec(memory_space=pltpu.VMEM), pl.BlockSpec(memory_space=pl.ANY)
SMEM = pl.BlockSpec(memory_space=pltpu.SMEM)

PROJECTION, TEXTS = 160, 32


def params(mebibytes):
    return pltpu.CompilerParams(vmem_limit_bytes=mebibytes * 1024 * 1024)


def normalize(values):
    values = values.astype(f32)
    center = jnp.mean(values, axis=-1, keepdims=True)
    spread = jnp.mean((values - center) ** 2, axis=-1, keepdims=True)
    return (values - center) / jnp.sqrt(spread + 1e-05)


def unit_rows(emb):
    square = jnp.sum(emb * emb, axis=1, keepdims=True)
    return (emb / jnp.sqrt(square + 1e-06)).astype(bf16)


def fetch(source, target, sem):
    copy = pltpu.make_async_copy(source, target, sem)
    copy.start()
    return copy


def fetch_rows(held, start, target, sem):
    count = target.shape[0] // 8
    return [
        fetch(
            held[i // 4].at[i % 4, pl.ds(start, count), :], target.at[pl.ds(i * count, count), :], sem
        )
        for i in range(8)
    ]


def texts_kernel(place_ref, mine, other, units_ref, proj, texts, sem):
    y, x, c = place_ref[0], place_ref[1], place_ref[2]
    count, width = units_ref.shape

    @pl.when(y >= 2)
    def _():
        held = (mine, other)
        for copy in fetch_rows(held, 0, proj, sem) + fetch_rows(held, PROJECTION, texts, sem):
            copy.wait()
        emb = lax.dot_general(texts[:, :width], proj[:, :width], NT, preferred_element_type=f32)
        place = lax.broadcasted_iota(jnp.int32, (count, count), 1)
        from_c = ((place >> 7) + c) & 1
        from_x = (x + 4 + (2 * from_c - 1) * ((place >> 5) & 3)) & 3
        index = ((place >> 1) & 7) * 32 + from_x * 8 + from_c * 4 + ((place >> 4) & 1) * 2 + (place & 1)
        order = (index == lax.broadcasted_iota(jnp.int32, (count, count), 0)).astype(bf16)
        units_ref[...] = jnp.dot(order, unit_rows(emb), preferred_element_type=f32).astype(bf16)


def text_units(place, mine, other, count, text_width):
    width = mine.shape[-1]
    rows = 8 * PROJECTION
    return pl.pallas_call(
        texts_kernel,
        out_shape=(
            jax.ShapeDtypeStruct((count, text_width), bf16),
            jax.ShapeDtypeStruct((rows, width), bf16),
        ),
        in_specs=[SMEM, ANYWHERE, ANYWHERE],
        out_specs=(VMEM, VMEM),
        scratch_shapes=[pltpu.VMEM((8 * TEXTS, width), bf16), pltpu.SemaphoreType.DMA],
        compiler_params=params(24),
        cost_estimate=pl.CostEstimate(
            flops=2 * count * text_width * rows, bytes_accessed=2 * rows * width, transcendentals=0
        ),
    )(place, mine, other)


def layer_step(layer, act, weights, normed):
    width = act.shape[1]
    normed[...] = normalize(act[...]).astype(bf16)
    for start in range(0, width, 256):
        cols = pl.ds(start, min(256, width - start))
        update = jnp.dot(normed[...], weights[layer, :, cols], preferred_element_type=f32)
        act[:, cols] = (act[:, cols].astype(f32) + jax.nn.gelu(update)).astype(bf16)


def layers_kernel(plane, y_ref, act_ref, weights, out_ref, normed):
    out_ref[...] = act_ref[...]

    @pl.when(y_ref[0] == plane)
    def _():
        for layer in range(2):
            layer_step(layer, out_ref, weights, normed)


def two_layers(plane, y, act, weights):
    tokens, width = act.shape
    return pl.pallas_call(
        functools.partial(layers_kernel, plane),
        out_shape=jax.ShapeDtypeStruct(act.shape, bf16),
        in_specs=[SMEM, VMEM, VMEM],
        out_specs=VMEM,
        scratch_shapes=[pltpu.VMEM(act.shape, bf16)],
        compiler_params=params(24),
        cost_estimate=pl.CostEstimate(
            flops=4 * tokens * width * width, bytes_accessed=4 * width * width, transcendentals=0
        ),
    )(y, act, weights)


def rows_kernel(tokens, y_ref, scale_ref, act_ref, weights, one, two, three, proj, units, rows_ref, act, normed):
    layers_kernel(3, y_ref, act_ref, weights, act, normed)

    @pl.when(y_ref[0] == 3)
    def _():
        sums = [jnp.sum(normalize(part[...]), axis=0, keepdims=True) for part in (act, one, two, three)]
        row = lax.broadcasted_iota(jnp.int32, (16, act.shape[1]), 0)
        pooled = jnp.where(row == 0, sums[0] + sums[1], sums[2] + sums[3])
        pooled = (pooled / tokens).astype(bf16)
        emb = lax.dot_general(pooled, proj[...], NT, preferred_element_type=f32)
        rows_ref[...] = scale_ref[0] * lax.dot_general(
            unit_rows(emb), units[...], NT, preferred_element_type=f32
        )


def logit_rows(y, scale, acts, weights, proj, units, tokens):
    act = acts[0]
    return pl.pallas_call(
        functools.partial(rows_kernel, tokens),
        out_shape=jax.ShapeDtypeStruct((16, units.shape[0]), f32),
        in_specs=[SMEM, SMEM] + [VMEM] * 7,
        out_specs=VMEM,
        scratch_shapes=[pltpu.VMEM(act.shape, bf16)] * 2,
        compiler_params=params(24),
    )(y, scale, act, weights, *acts[1:], proj, units)[:2]


def hop(value):
    return lax.ppermute(
        value, ("x", "c"),
        [(i * 2 + c, (i + 1 - 2 * c) % 4 * 2 + c) for i in range(4) for c in range(2)],
    )


def on_device(images, text_pooled, image_weight, proj_image, proj_text, logit_scale, pairing):
    y, zh, zl, x, c = (lax.axis_index(name) for name in AXES)
    width, text_width = proj_image.shape[0], proj_text.shape[0]
    micro = images.shape[0]
    count = pairing.shape[0]

    half = proj_image.shape[1] // 2
    widen = ((0, 0), (0, width - text_width))
    projection = jnp.where(
        y == 3,
        lax.dynamic_slice_in_dim(proj_image, zh * half, half, 1).T,
        jnp.pad(lax.dynamic_slice_in_dim(proj_text, zh * half, half, 1).T, widen),
    )
    texts = jnp.pad(lax.dynamic_slice_in_dim(text_pooled, zh * 2, 2, 0), widen)
    rows = lax.all_gather(image_weight[0], ("x", "c"), axis=0).reshape(-1, width)
    half_rows = rows.shape[0] // 2
    rows = jnp.where(c == 0, rows[:half_rows], rows[half_rows:])
    rows, projection, texts = lax.optimization_barrier((rows, projection, texts))
    weights = lax.all_gather(rows, Z + ("c",), axis=0, tiled=True)

    ring = lax.all_gather(jnp.concatenate([projection, texts]), Z, axis=0)
    line = [jnp.concatenate([
        ring[:, :half].reshape(PROJECTION, width), ring[:, half:].reshape(TEXTS, width)
    ])]
    for _ in range(3):
        line.append(hop(line[-1]))
    mine = jnp.stack(line)
    other = lax.ppermute(mine, "c", [(0, 1), (1, 0)])
    weights, mine, other = lax.optimization_barrier((weights, mine, other))
    weights = weights.reshape(2, width, width)
    place = jnp.stack([y, x, c]).astype(jnp.int32)
    units, projection = text_units(place, mine, other, count, text_width)
    units = lax.ppermute(units, "y", [(2, 3)])

    part = images.shape[1] // 2
    acts = [
        lax.dynamic_slice(images, (zh * 2 + i, j * part, 0), (1, part, width))[0]
        for i in range(2) for j in range(2)
    ]
    turn = y.astype(jnp.int32)[None]
    for plane in range(3):
        for i in range(4):
            acts[i] = lax.ppermute(two_layers(plane, turn, acts[i], weights), "y", [(plane, plane + 1)])
        if plane == 1:
            acts[3], units = lax.optimization_barrier((acts[3], units))
    acts[1:] = [two_layers(3, turn, act, weights) for act in acts[1:]]
    own_rows = logit_rows(turn, logit_scale, acts, weights, projection, units, images.shape[1])

    of_z = lax.all_to_all(jnp.broadcast_to(own_rows[None], (16, 2, count)), Z, 0, 0, tiled=True)
    by_place = of_z.reshape(2, 8, 2, count)
    zero = jnp.int32(0)
    of_dp = lax.dynamic_slice(by_place, (zero, zl, zero, zero), (2, 1, 2, count)).reshape(micro, count)
    sums = jnp.sum(jnp.exp(of_z), axis=(0, 1))
    sent = jnp.concatenate([of_dp, sums[None]])
    from_plane = lax.all_to_all(
        jnp.broadcast_to(sent[None], (16,) + sent.shape), ("y", "x"), 0, 0, tiled=True
    )[12:]
    own_logits = lax.dynamic_index_in_dim(from_plane, x, 0, False)[:micro]
    column_lse = jnp.log(lax.psum(jnp.sum(from_plane[:, micro], axis=0), "c"))
    row_start = ((zl * 4 + x) * 2 + c) * micro
    own_pairs = lax.dynamic_slice_in_dim(pairing, row_start, micro, 0)
    paired = own_pairs[:, None] == lax.broadcasted_iota(jnp.int32, (1, count), 1)
    positive = jnp.sum(jnp.where(paired, own_logits, 0.0), axis=1)
    image_loss = jnp.log(jnp.sum(jnp.exp(own_logits), axis=1)) - positive
    text_loss = jnp.sum(jnp.where(paired, column_lse[None, :], 0.0), axis=1) - positive
    columns = count // 8
    logit_block = lax.dynamic_slice_in_dim(own_logits, (y * 2 + zh) * columns, columns, 1)
    return (logit_block, image_loss, text_loss)


def solution(mesh):
    fine = Mesh(mesh.devices.reshape(SIZES), AXES)
    section, dp = ("y", "zh"), ("zl", "x", "c")
    in_specs = (
        P(dp, None, None),
        P(dp, None),
        P(section, dp, None),
        P(None, dp),
        P(None, dp),
        P(),
        P(),
    )
    out_specs = (P(dp, section), P(dp), P(dp))
    return jax.shard_map(on_device, mesh=fine, in_specs=in_specs, out_specs=out_specs, check_vma=False)
```

```python
import functools

import jax
import jax.numpy as jnp
from jax import lax
from jax.experimental import pallas as pl
from jax.experimental.pallas import tpu as pltpu
from jax.sharding import Mesh, PartitionSpec as P

AXES = ("y", "zh", "zl", "x", "c")
SIZES = (4, 2, 8, 4, 2)
Z = ("zh", "zl")
NT = (((1,), (1,)), ((), ()))
bf16, f32 = jnp.bfloat16, jnp.float32
VMEM, ANYWHERE = pl.BlockSpec(memory_space=pltpu.VMEM), pl.BlockSpec(memory_space=pl.ANY)
SMEM = pl.BlockSpec(memory_space=pltpu.SMEM)

PROJECTION, TEXTS = 160, 32


def params(mebibytes):
    return pltpu.CompilerParams(vmem_limit_bytes=mebibytes * 1024 * 1024)


def normalize(values):
    values = values.astype(f32)
    center = jnp.mean(values, axis=-1, keepdims=True)
    spread = jnp.mean((values - center) ** 2, axis=-1, keepdims=True)
    return (values - center) / jnp.sqrt(spread + 1e-05)


def unit_rows(emb):
    square = jnp.sum(emb * emb, axis=1, keepdims=True)
    return (emb / jnp.sqrt(square + 1e-06)).astype(bf16)


def fetch(source, target, sem):
    copy = pltpu.make_async_copy(source, target, sem)
    copy.start()
    return copy


def fetch_rows(held, start, target, sem):
    count = target.shape[0] // 8
    return [
        fetch(
            held[i // 4].at[i % 4, pl.ds(start, count), :], target.at[pl.ds(i * count, count), :], sem
        )
        for i in range(8)
    ]


def texts_kernel(place_ref, mine, other, units_ref, proj, texts, sem):
    y, x, c = place_ref[0], place_ref[1], place_ref[2]
    count, width = units_ref.shape

    @pl.when(y >= 2)
    def _():
        held = (mine, other)
        for copy in fetch_rows(held, 0, proj, sem) + fetch_rows(held, PROJECTION, texts, sem):
            copy.wait()
        emb = lax.dot_general(texts[:, :width], proj[:, :width], NT, preferred_element_type=f32)
        place = lax.broadcasted_iota(jnp.int32, (count, count), 1)
        from_c = ((place >> 7) + c) & 1
        from_x = (x + 4 + (2 * from_c - 1) * ((place >> 5) & 3)) & 3
        index = ((place >> 1) & 7) * 32 + from_x * 8 + from_c * 4 + ((place >> 4) & 1) * 2 + (place & 1)
        order = (index == lax.broadcasted_iota(jnp.int32, (count, count), 0)).astype(bf16)
        units_ref[...] = jnp.dot(order, unit_rows(emb), preferred_element_type=f32).astype(bf16)


def text_units(place, mine, other, count, text_width):
    width = mine.shape[-1]
    rows = 8 * PROJECTION
    return pl.pallas_call(
        texts_kernel,
        out_shape=(
            jax.ShapeDtypeStruct((count, text_width), bf16),
            jax.ShapeDtypeStruct((rows, width), bf16),
        ),
        in_specs=[SMEM, ANYWHERE, ANYWHERE],
        out_specs=(VMEM, VMEM),
        scratch_shapes=[pltpu.VMEM((8 * TEXTS, width), bf16), pltpu.SemaphoreType.DMA],
        compiler_params=params(24),
        cost_estimate=pl.CostEstimate(
            flops=2 * count * text_width * rows, bytes_accessed=2 * rows * width, transcendentals=0
        ),
    )(place, mine, other)


def layer_step(layer, act, weights, normed):
    width = act.shape[1]
    normed[...] = normalize(act[...]).astype(bf16)
    for start in range(0, width, 256):
        cols = pl.ds(start, min(256, width - start))
        update = jnp.dot(normed[...], weights[layer, :, cols], preferred_element_type=f32)
        act[:, cols] = (act[:, cols].astype(f32) + jax.nn.gelu(update)).astype(bf16)


def layers_kernel(plane, y_ref, act_ref, weights, out_ref, normed):
    out_ref[...] = act_ref[...]

    @pl.when(y_ref[0] == plane)
    def _():
        for layer in range(2):
            layer_step(layer, out_ref, weights, normed)


def token_sum(act):
    return jnp.sum(normalize(act[...]), axis=0, keepdims=True)


def sums_kernel(y_ref, act_ref, weights, out_ref, act, normed):
    layers_kernel(3, y_ref, act_ref, weights, act, normed)

    @pl.when(y_ref[0] == 3)
    def _():
        out_ref[...] = jnp.broadcast_to(token_sum(act), out_ref.shape)


def two_layers(plane, y, act, weights):
    tokens, width = act.shape
    last = plane == 3
    scratch = pltpu.VMEM(act.shape, bf16)
    return pl.pallas_call(
        sums_kernel if last else functools.partial(layers_kernel, plane),
        out_shape=jax.ShapeDtypeStruct((8, width), f32) if last else jax.ShapeDtypeStruct(act.shape, bf16),
        in_specs=[SMEM, VMEM, VMEM],
        out_specs=VMEM,
        scratch_shapes=[scratch] * (2 if last else 1),
        compiler_params=params(24),
        cost_estimate=pl.CostEstimate(
            flops=4 * tokens * width * width, bytes_accessed=4 * width * width, transcendentals=0
        ),
    )(y, act, weights)


def rows_kernel(tokens, y_ref, scale_ref, act_ref, weights, one, two, three, proj, units, rows_ref, act, normed):
    layers_kernel(3, y_ref, act_ref, weights, act, normed)

    @pl.when(y_ref[0] == 3)
    def _():
        row = lax.broadcasted_iota(jnp.int32, (16, act.shape[1]), 0)
        pooled = jnp.where(row == 0, token_sum(act) + one[:1], two[:1] + three[:1])
        pooled = (pooled / tokens).astype(bf16)
        emb = lax.dot_general(pooled, proj[...], NT, preferred_element_type=f32)
        rows_ref[...] = scale_ref[0] * lax.dot_general(
            unit_rows(emb), units[...], NT, preferred_element_type=f32
        )


def logit_rows(y, scale, act, sums, weights, proj, units, tokens):
    return pl.pallas_call(
        functools.partial(rows_kernel, tokens),
        out_shape=jax.ShapeDtypeStruct((16, units.shape[0]), f32),
        in_specs=[SMEM, SMEM] + [VMEM] * 7,
        out_specs=VMEM,
        scratch_shapes=[pltpu.VMEM(act.shape, bf16)] * 2,
        compiler_params=params(24),
    )(y, scale, act, weights, *sums, proj, units)[:2]


def hop(value):
    return lax.ppermute(
        value, ("x", "c"),
        [(i * 2 + c, (i + 1 - 2 * c) % 4 * 2 + c) for i in range(4) for c in range(2)],
    )


def on_device(images, text_pooled, image_weight, proj_image, proj_text, logit_scale, pairing):
    y, zh, zl, x, c = (lax.axis_index(name) for name in AXES)
    width, text_width = proj_image.shape[0], proj_text.shape[0]
    micro = images.shape[0]
    count = pairing.shape[0]

    half = proj_image.shape[1] // 2
    widen = ((0, 0), (0, width - text_width))
    projection = jnp.where(
        y == 3,
        lax.dynamic_slice_in_dim(proj_image, zh * half, half, 1).T,
        jnp.pad(lax.dynamic_slice_in_dim(proj_text, zh * half, half, 1).T, widen),
    )
    texts = jnp.pad(lax.dynamic_slice_in_dim(text_pooled, zh * 2, 2, 0), widen)
    rows = lax.all_gather(image_weight[0], ("x", "c"), axis=0).reshape(-1, width)
    half_rows = rows.shape[0] // 2
    rows = jnp.where(c == 0, rows[:half_rows], rows[half_rows:])
    rows, projection, texts = lax.optimization_barrier((rows, projection, texts))
    weights = lax.all_gather(rows, Z + ("c",), axis=0, tiled=True)

    ring = lax.all_gather(jnp.concatenate([projection, texts]), Z, axis=0)
    line = [jnp.concatenate([
        ring[:, :half].reshape(PROJECTION, width), ring[:, half:].reshape(TEXTS, width)
    ])]
    for _ in range(3):
        line.append(hop(line[-1]))
    mine = jnp.stack(line)
    other = lax.ppermute(mine, "c", [(0, 1), (1, 0)])
    weights, mine, other = lax.optimization_barrier((weights, mine, other))
    weights = weights.reshape(2, width, width)
    place = jnp.stack([y, x, c]).astype(jnp.int32)
    units, projection = text_units(place, mine, other, count, text_width)
    units = lax.ppermute(units, "y", [(2, 3)])

    part = images.shape[1] // 2
    acts = [
        lax.dynamic_slice(images, (zh * 2 + i, j * part, 0), (1, part, width))[0]
        for i in range(2) for j in range(2)
    ]
    turn = y.astype(jnp.int32)[None]
    for plane in range(3):
        for i in range(4):
            acts[i] = lax.ppermute(two_layers(plane, turn, acts[i], weights), "y", [(plane, plane + 1)])
        if plane == 1:
            acts[3], units = lax.optimization_barrier((acts[3], units))
    sums = [two_layers(3, turn, act, weights) for act in acts[1:]]
    own_rows = logit_rows(turn, logit_scale, acts[0], sums, weights, projection, units, images.shape[1])

    of_z = lax.all_to_all(jnp.broadcast_to(own_rows[None], (16, 2, count)), Z, 0, 0, tiled=True)
    by_place = of_z.reshape(2, 8, 2, count)
    zero = jnp.int32(0)
    of_dp = lax.dynamic_slice(by_place, (zero, zl, zero, zero), (2, 1, 2, count)).reshape(micro, count)
    sums = jnp.sum(jnp.exp(of_z), axis=(0, 1))
    sent = jnp.concatenate([of_dp, sums[None]])
    from_plane = lax.all_to_all(
        jnp.broadcast_to(sent[None], (16,) + sent.shape), ("y", "x"), 0, 0, tiled=True
    )[12:]
    own_logits = lax.dynamic_index_in_dim(from_plane, x, 0, False)[:micro]
    column_lse = jnp.log(lax.psum(jnp.sum(from_plane[:, micro], axis=0), "c"))
    row_start = ((zl * 4 + x) * 2 + c) * micro
    own_pairs = lax.dynamic_slice_in_dim(pairing, row_start, micro, 0)
    paired = own_pairs[:, None] == lax.broadcasted_iota(jnp.int32, (1, count), 1)
    positive = jnp.sum(jnp.where(paired, own_logits, 0.0), axis=1)
    image_loss = jnp.log(jnp.sum(jnp.exp(own_logits), axis=1)) - positive
    text_loss = jnp.sum(jnp.where(paired, column_lse[None, :], 0.0), axis=1) - positive
    columns = count // 8
    logit_block = lax.dynamic_slice_in_dim(own_logits, (y * 2 + zh) * columns, columns, 1)
    return (logit_block, image_loss, text_loss)


def solution(mesh):
    fine = Mesh(mesh.devices.reshape(SIZES), AXES)
    section, dp = ("y", "zh"), ("zl", "x", "c")
    in_specs = (
        P(dp, None, None),
        P(dp, None),
        P(section, dp, None),
        P(None, dp),
        P(None, dp),
        P(),
        P(),
    )
    out_specs = (P(dp, section), P(dp), P(dp))
    return jax.shard_map(on_device, mesh=fine, in_specs=in_specs, out_specs=out_specs, check_vma=False)
```

```python
import functools

import jax
import jax.numpy as jnp
from jax import lax
from jax.experimental import pallas as pl
from jax.experimental.pallas import tpu as pltpu
from jax.sharding import Mesh, PartitionSpec as P

AXES = ("y", "zh", "zl", "x", "c")
SIZES = (4, 2, 8, 4, 2)
Z = ("zh", "zl")
NT = (((1,), (1,)), ((), ()))
bf16, f32 = jnp.bfloat16, jnp.float32
VMEM, ANYWHERE = pl.BlockSpec(memory_space=pltpu.VMEM), pl.BlockSpec(memory_space=pl.ANY)
SMEM = pl.BlockSpec(memory_space=pltpu.SMEM)

PROJECTION, TEXTS = 160, 32


def params(mebibytes):
    return pltpu.CompilerParams(vmem_limit_bytes=mebibytes * 1024 * 1024)


def normalize(values):
    values = values.astype(f32)
    center = jnp.mean(values, axis=-1, keepdims=True)
    spread = jnp.mean((values - center) ** 2, axis=-1, keepdims=True)
    return (values - center) / jnp.sqrt(spread + 1e-05)


def unit_rows(emb):
    square = jnp.sum(emb * emb, axis=1, keepdims=True)
    return (emb / jnp.sqrt(square + 1e-06)).astype(bf16)


def fetch(source, target, sem):
    copy = pltpu.make_async_copy(source, target, sem)
    copy.start()
    return copy


def fetch_rows(held, start, target, sem):
    count = target.shape[0] // 8
    return [
        fetch(
            held[i // 4].at[i % 4, pl.ds(start, count), :], target.at[pl.ds(i * count, count), :], sem
        )
        for i in range(8)
    ]


def texts_kernel(place_ref, mine, other, units_ref, proj, texts, sem):
    y, x, c = place_ref[0], place_ref[1], place_ref[2]
    count, width = units_ref.shape

    @pl.when(y >= 2)
    def _():
        held = (mine, other)
        for copy in fetch_rows(held, 0, proj, sem) + fetch_rows(held, PROJECTION, texts, sem):
            copy.wait()
        emb = lax.dot_general(texts[:, :width], proj[:, :width], NT, preferred_element_type=f32)
        place = lax.broadcasted_iota(jnp.int32, (count, count), 1)
        from_c = ((place >> 7) + c) & 1
        from_x = (x + 4 + (2 * from_c - 1) * ((place >> 5) & 3)) & 3
        index = ((place >> 1) & 7) * 32 + from_x * 8 + from_c * 4 + ((place >> 4) & 1) * 2 + (place & 1)
        order = (index == lax.broadcasted_iota(jnp.int32, (count, count), 0)).astype(bf16)
        units_ref[...] = jnp.dot(order, unit_rows(emb), preferred_element_type=f32).astype(bf16)


def text_units(place, mine, other, count, text_width):
    width = mine.shape[-1]
    rows = 8 * PROJECTION
    return pl.pallas_call(
        texts_kernel,
        out_shape=(
            jax.ShapeDtypeStruct((count, text_width), bf16),
            jax.ShapeDtypeStruct((rows, width), bf16),
        ),
        in_specs=[SMEM, ANYWHERE, ANYWHERE],
        out_specs=(VMEM, VMEM),
        scratch_shapes=[pltpu.VMEM((8 * TEXTS, width), bf16), pltpu.SemaphoreType.DMA],
        compiler_params=params(24),
        cost_estimate=pl.CostEstimate(
            flops=2 * count * text_width * rows, bytes_accessed=2 * rows * width, transcendentals=0
        ),
    )(place, mine, other)


def layer_step(layer, act, weights, normed):
    width = act.shape[1]
    normed[...] = normalize(act[...]).astype(bf16)
    for start in range(0, width, 256):
        cols = pl.ds(start, min(256, width - start))
        update = jnp.dot(normed[...], weights[layer, :, cols], preferred_element_type=f32)
        act[:, cols] = (act[:, cols].astype(f32) + jax.nn.gelu(update)).astype(bf16)


def layers_kernel(plane, y_ref, act_ref, weights, out_ref, normed):
    out_ref[...] = act_ref[...]

    @pl.when(y_ref[0] == plane)
    def _():
        for layer in range(2):
            layer_step(layer, out_ref, weights, normed)


def token_sum(act):
    return jnp.sum(normalize(act[...]), axis=0, keepdims=True)


def sums_kernel(y_ref, act_ref, weights, out_ref, act, normed):
    layers_kernel(3, y_ref, act_ref, weights, act, normed)

    @pl.when(y_ref[0] == 3)
    def _():
        out_ref[...] = jnp.broadcast_to(token_sum(act), out_ref.shape)


def two_layers(plane, y, act, weights):
    tokens, width = act.shape
    last = plane == 3
    scratch = pltpu.VMEM(act.shape, bf16)
    return pl.pallas_call(
        sums_kernel if last else functools.partial(layers_kernel, plane),
        out_shape=jax.ShapeDtypeStruct((8, width), f32) if last else jax.ShapeDtypeStruct(act.shape, bf16),
        in_specs=[SMEM, VMEM, VMEM],
        out_specs=VMEM,
        scratch_shapes=[scratch] * (2 if last else 1),
        compiler_params=params(24),
        cost_estimate=pl.CostEstimate(
            flops=4 * tokens * width * width, bytes_accessed=4 * width * width, transcendentals=0
        ),
    )(y, act, weights)


def rows_kernel(tokens, y_ref, scale_ref, act_ref, weights, one, two, three, proj, units, rows_ref, act, normed):
    layers_kernel(3, y_ref, act_ref, weights, act, normed)

    @pl.when(y_ref[0] == 3)
    def _():
        row = lax.broadcasted_iota(jnp.int32, (16, act.shape[1]), 0)
        pooled = jnp.where(row == 0, token_sum(act) + one[:1], two[:1] + three[:1])
        pooled = (pooled / tokens).astype(bf16)
        emb = lax.dot_general(pooled, proj[...], NT, preferred_element_type=f32)
        rows_ref[...] = scale_ref[0] * lax.dot_general(
            unit_rows(emb), units[...], NT, preferred_element_type=f32
        )


def logit_rows(y, scale, act, sums, weights, proj, units, tokens):
    return pl.pallas_call(
        functools.partial(rows_kernel, tokens),
        out_shape=jax.ShapeDtypeStruct((16, units.shape[0]), f32),
        in_specs=[SMEM, SMEM] + [VMEM] * 7,
        out_specs=VMEM,
        scratch_shapes=[pltpu.VMEM(act.shape, bf16)] * 2,
        compiler_params=params(24),
    )(y, scale, act, weights, *sums, proj, units)[:2]


def hop(value):
    return lax.ppermute(
        value, ("x", "c"),
        [(i * 2 + c, (i + 1 - 2 * c) % 4 * 2 + c) for i in range(4) for c in range(2)],
    )


def on_device(images, text_pooled, image_weight, proj_image, proj_text, logit_scale, pairing):
    y, zh, zl, x, c = (lax.axis_index(name) for name in AXES)
    width, text_width = proj_image.shape[0], proj_text.shape[0]
    micro = images.shape[0]
    count = pairing.shape[0]

    half = proj_image.shape[1] // 2
    widen = ((0, 0), (0, width - text_width))
    projection = jnp.where(
        y == 3,
        lax.dynamic_slice_in_dim(proj_image, zh * half, half, 1).T,
        jnp.pad(lax.dynamic_slice_in_dim(proj_text, zh * half, half, 1).T, widen),
    )
    texts = jnp.pad(lax.dynamic_slice_in_dim(text_pooled, zh * 2, 2, 0), widen)
    rows = lax.all_gather(image_weight[0], ("x", "c"), axis=0).reshape(-1, width)
    half_rows = rows.shape[0] // 2
    rows = jnp.where(c == 0, rows[:half_rows], rows[half_rows:])
    rows, projection, texts = lax.optimization_barrier((rows, projection, texts))
    weights = lax.all_gather(rows, Z + ("c",), axis=0, tiled=True)

    ring = lax.all_gather(jnp.concatenate([projection, texts]), Z, axis=0)
    line = [jnp.concatenate([
        ring[:, :half].reshape(PROJECTION, width), ring[:, half:].reshape(TEXTS, width)
    ])]
    for _ in range(3):
        line.append(hop(line[-1]))
    mine = jnp.stack(line)
    other = lax.ppermute(mine, "c", [(0, 1), (1, 0)])
    weights, mine, other = lax.optimization_barrier((weights, mine, other))
    weights = weights.reshape(2, width, width)
    place = jnp.stack([y, x, c]).astype(jnp.int32)
    units, projection = text_units(place, mine, other, count, text_width)
    units = lax.ppermute(units, "y", [(2, 3)])

    part = images.shape[1] // 2
    acts = [
        lax.dynamic_slice(images, (zh * 2 + i, j * part, 0), (1, part, width))[0]
        for i in range(2) for j in range(2)
    ]
    turn = y.astype(jnp.int32)[None]
    for plane in range(3):
        for i in range(4):
            acts[i] = lax.ppermute(two_layers(plane, turn, acts[i], weights), "y", [(plane, plane + 1)])
        if plane == 1:
            acts[3], units = lax.optimization_barrier((acts[3], units))
    sums = [two_layers(3, turn, act, weights) for act in acts[1:]]
    own_rows = logit_rows(turn, logit_scale, acts[0], sums, weights, projection, units, images.shape[1])

    of_z = lax.all_to_all(
        jnp.broadcast_to(own_rows[None], (32, 2, count)), Z + ("c",), 0, 0, tiled=True
    )
    by_place = of_z.reshape(2, 8, 2, 2, count)
    zero = jnp.int32(0)
    of_dp = lax.dynamic_slice(
        by_place, (zero, zl, c, zero, zero), (2, 1, 1, 2, count)
    ).reshape(micro, count)
    sums = jnp.sum(jnp.exp(of_z), axis=(0, 1))
    sent = jnp.concatenate([of_dp, sums[None]])
    from_plane = lax.all_to_all(
        jnp.broadcast_to(sent[None], (16,) + sent.shape), ("y", "x"), 0, 0, tiled=True
    )[12:]
    own_logits = lax.dynamic_index_in_dim(from_plane, x, 0, False)[:micro]
    column_lse = jnp.log(jnp.sum(from_plane[:, micro], axis=0))
    row_start = ((zl * 4 + x) * 2 + c) * micro
    own_pairs = lax.dynamic_slice_in_dim(pairing, row_start, micro, 0)
    paired = own_pairs[:, None] == lax.broadcasted_iota(jnp.int32, (1, count), 1)
    positive = jnp.sum(jnp.where(paired, own_logits, 0.0), axis=1)
    image_loss = jnp.log(jnp.sum(jnp.exp(own_logits), axis=1)) - positive
    text_loss = jnp.sum(jnp.where(paired, column_lse[None, :], 0.0), axis=1) - positive
    columns = count // 8
    logit_block = lax.dynamic_slice_in_dim(own_logits, (y * 2 + zh) * columns, columns, 1)
    return (logit_block, image_loss, text_loss)


def solution(mesh):
    fine = Mesh(mesh.devices.reshape(SIZES), AXES)
    section, dp = ("y", "zh"), ("zl", "x", "c")
    in_specs = (
        P(dp, None, None),
        P(dp, None),
        P(section, dp, None),
        P(None, dp),
        P(None, dp),
        P(),
        P(),
    )
    out_specs = (P(dp, section), P(dp), P(dp))
    return jax.shard_map(on_device, mesh=fine, in_specs=in_specs, out_specs=out_specs, check_vma=False)
```
